256 devices in a mesh: fsdp: 32 (over z, y_hi, core), tp: 8 (over y_lo, x).
Axes of the slice: x: 4, y: 4 (y_hi: 2, y_lo: 2; y = y_hi * 2 + y_lo), z: 8, core: 2. Of those that a mesh axis runs over, the one named last changes fastest.
Arguments:
- train_x: bfloat16 [32768, 8192], P('fsdp'), may hold values from -6 to 6
- train_q: bfloat16 [32768, 8192], P('fsdp', 'tp'), may hold values from -17 to 17
- train_k: bfloat16 [32768, 1024], P('fsdp', 'tp'), may hold values from -14 to 14
- train_target: bfloat16 [32768, 8192], P('fsdp', 'tp'), may hold values from -6 to 6
- train_skill: int32 [128], replicated, may hold values from 0 to 3, as said below
- value_weight: bfloat16 [8192, 1024], P('fsdp', 'tp'), may hold values from -0.0625 to 0.0625
- val_x: bfloat16 [4096, 8192], P('fsdp'), may hold values from -6 to 6
- val_q: bfloat16 [4096, 8192], P('fsdp', 'tp'), may hold values from -17 to 17
- val_k: bfloat16 [4096, 1024], P('fsdp', 'tp'), may hold values from -14 to 14
- val_target: bfloat16 [4096, 8192], P('fsdp', 'tp'), may hold values from -6 to 6
- val_skill: int32 [32], replicated, may hold values from 0 to 3, as said below
Outputs:
- skill_grads: bfloat16 [4, 8192, 1024], P(None, 'fsdp', 'tp')
- transfer: float32 [4, 4], replicated
The draws below stay inside these ranges and needn't reach their ends.
Inputs may be any that keep to these rules, and one draw needn't show every extreme that they name: `train_skill`: each of the 4 skills labels exactly 32 sequences. `val_skill`: each of the 4 skills labels exactly 8 sequences.
All inputs are finite; a program needn't handle non-finite values.
Results may differ from the reference program's by a relative error of at most 0.0052.
The reference program's roundings to bfloat16 on the way count: a program that leaves them out, or rounds other values in their place, can miss the bound.
Values may be sent and summed in bfloat16 or wider, within the bound.
No kernel may reach another device: no remote copies, remote signals or barrier semaphores. Data moves between devices by JAX's collectives and lax.ppermute only.
A program may use at most 192 MiB of HBM per device.

```python
import math
import jax
import jax.numpy as jnp
from jax import lax

D = 8192
HQ = 64
KVH = 8
HD = 128
SKILLS = 4
SEQ = 256
VSEQ = 128
TRAIN_SEQS = 128
VAL_SEQS = 32
TRAIN_TOKENS = 32768
VAL_TOKENS = 4096


def drawn_pair(key, rows):
    key_query, key_keys = jax.random.split(key, 2)
    queries = jax.random.truncated_normal(key_query, -4.0, 4.0, (rows, HQ * HD), jnp.float32)
    keys = jax.random.truncated_normal(key_keys, -4.0, 4.0, (rows, KVH * HD), jnp.float32)
    return (queries, keys)


def draw_train_q(key, part):
    return drawn_pair(jax.random.fold_in(key, 31), TRAIN_TOKENS)[0].astype(jnp.bfloat16)


def draw_train_k(key, part):
    return drawn_pair(jax.random.fold_in(key, 31), TRAIN_TOKENS)[1].astype(jnp.bfloat16)


def draw_val_q(key, part):
    return drawn_pair(jax.random.fold_in(key, 47), VAL_TOKENS)[0].astype(jnp.bfloat16)


def draw_val_k(key, part):
    return drawn_pair(jax.random.fold_in(key, 47), VAL_TOKENS)[1].astype(jnp.bfloat16)


def draw_train_skill(key, part):
    shuffled = jax.random.permutation(jax.random.fold_in(key, 5), TRAIN_SEQS)
    return (shuffled % SKILLS).astype(jnp.int32)


def draw_val_skill(key, part):
    shuffled = jax.random.permutation(jax.random.fold_in(key, 9), VAL_SEQS)
    return (shuffled % SKILLS).astype(jnp.int32)


def strengthened(entries, own_key, source, target, shards_of, factor):
    owner, partner = [(jnp.arange(entries.shape[position]) // (entries.shape[position] // shards_of)).reshape([-1 if axis == position else 1 for axis in range(entries.ndim)]) for position in (source, target)]
    chosen = jax.random.permutation(own_key, shards_of)[partner]
    strong = (owner == chosen) | (owner == (partner + shards_of // 2) % shards_of)
    return jnp.where(strong, factor * entries, entries)


def block_scale(key, dims, shards, smallest, top_value):
    loudness, own = 1.0, jax.random.fold_in(key, 6)
    for position, parts in shards:
        steps = jnp.exp(jax.random.uniform(jax.random.fold_in(own, position), (parts,), jnp.float32, smallest / len(shards), top_value / len(shards)))
        loudness = loudness * jnp.repeat(steps, dims[position] // parts).reshape([-1 if axis == position else 1 for axis in range(len(dims))])
    return loudness


def bell_draw(key, extent, scale, most, shards=(), kind=jnp.bfloat16):
    values = jax.random.normal(key, extent, jnp.float32) * scale
    if len(shards) > 0:
        values = block_scale(key, extent, shards, -0.22, 0.18) * values
    return jnp.clip(values, min=-most, max=most).astype(kind)


def bell_draw_with(own_key, dims, width, limit, cuts, heavy, kind=jnp.bfloat16):
    values = width * jax.random.normal(own_key, dims, jnp.float32)
    if cuts:
        values = values * block_scale(own_key, dims, cuts, -0.22, 0.18)
    return jnp.clip(strengthened(values, jax.random.fold_in(own_key, 3), *heavy), -limit, limit).astype(kind)


def setup_inputs(seed: int = 0) -> dict:
    key_of = jax.random.split(jax.random.key(seed), 12)
    train_x = bell_draw_with(key_of[0], (TRAIN_TOKENS, D), 1.0, 6.0, ((0, 32),), (0, 1, 32, 2.75))
    train_q = draw_train_q(jax.random.fold_in(key_of[11], 71), 0)
    train_k = draw_train_k(jax.random.fold_in(key_of[11], 71), 0)
    train_target = bell_draw(key_of[3], (TRAIN_TOKENS, HQ * HD), 1.0, 6.0, ((0, 32), (1, 8)))
    train_skill = draw_train_skill(jax.random.fold_in(key_of[11], 71), 0)
    value_weight = bell_draw(key_of[5], (D, KVH * HD), D ** -0.5, 0.0625, ((0, 32), (1, 8)))
    val_x = bell_draw(key_of[6], (VAL_TOKENS, D), 1.0, 6.0, ((0, 32),))
    val_q = draw_val_q(jax.random.fold_in(key_of[11], 71), 0)
    val_k = draw_val_k(jax.random.fold_in(key_of[11], 71), 0)
    val_target = bell_draw(key_of[9], (VAL_TOKENS, HQ * HD), 1.0, 6.0, ((0, 32), (1, 8)))
    val_skill = draw_val_skill(jax.random.fold_in(key_of[11], 71), 0)
    return {"train_x": train_x, "train_q": train_q, "train_k": train_k, "train_target": train_target, "train_skill": train_skill, "value_weight": value_weight, "val_x": val_x, "val_q": val_q, "val_k": val_k, "val_target": val_target, "val_skill": val_skill}


step_size = 0.01

def attend(query_rows, key_rows, length):
    kv_heads = key_rows.shape[1] // HD
    group = query_rows.shape[1] // HD // kv_heads
    queries = query_rows.reshape(length, kv_heads, group, HD).astype(jnp.float32)
    keys = key_rows.reshape(length, kv_heads, HD).astype(jnp.float32)
    scores = jnp.einsum('qgrh,kgh->grqk', queries, keys) * (1.0 / math.sqrt(HD))
    places = jnp.arange(length)
    allowed = places[:, None] >= places[None, :]
    scores = jnp.where(allowed, scores, jnp.float32(-1e+30))
    highest = lax.optimization_barrier(jnp.max(scores, axis=-1, keepdims=True))
    raised = jnp.exp(scores - highest)
    return (raised / lax.optimization_barrier(jnp.sum(raised, axis=-1, keepdims=True))).astype(jnp.bfloat16)

def mix_heads(attention, value_rows, length):
    kv_heads = attention.shape[0]
    blocks = value_rows.reshape(length, kv_heads, HD).astype(jnp.float32)
    mixed = jnp.einsum('grqk,kgh->qgrh', attention.astype(jnp.float32), blocks)
    return mixed

def reference(train_x, train_q, train_k, train_target, train_skill, value_weight, val_x, val_q, val_k, val_target, val_skill):
    head_width = value_weight.shape[1]
    values = jnp.dot(train_x, value_weight, preferred_element_type=jnp.float32).astype(jnp.bfloat16)
    val_values = jnp.dot(val_x, value_weight, preferred_element_type=jnp.float32).astype(jnp.bfloat16)

    def train_sequence(inputs):
        query_rows, key_rows, value_rows, target_rows = inputs
        attention = attend(query_rows, key_rows, SEQ)
        mixed = mix_heads(attention, value_rows, SEQ)
        target_blocks = target_rows.reshape(mixed.shape).astype(jnp.float32)
        residual = ((mixed - target_blocks) / SEQ).astype(jnp.bfloat16)
        pulled = jnp.einsum('grqk,qgrh->kgh', attention.astype(jnp.float32), residual.astype(jnp.float32))
        return pulled.reshape(SEQ, head_width).astype(jnp.bfloat16)
    value_grads = lax.map(train_sequence, (train_q.reshape(TRAIN_SEQS, SEQ, -1), train_k.reshape(TRAIN_SEQS, SEQ, -1), values.reshape(TRAIN_SEQS, SEQ, -1), train_target.reshape(TRAIN_SEQS, SEQ, -1)))
    order = jnp.argsort(train_skill, stable=True).astype(jnp.int32)
    per_skill = TRAIN_SEQS // SKILLS
    chosen = order.reshape(SKILLS, per_skill)
    input_seqs = train_x.reshape(TRAIN_SEQS, SEQ, D)

    def skill_gradient(rows):
        inputs_here = input_seqs[rows].reshape(per_skill * SEQ, D)
        grads_here = value_grads[rows].reshape(per_skill * SEQ, head_width)
        return jnp.dot(inputs_here.T, grads_here, preferred_element_type=jnp.float32).astype(jnp.bfloat16)
    skill_grads = lax.map(skill_gradient, chosen)

    def val_sequence(inputs):
        query_rows, key_rows, value_rows, target_rows = inputs
        attention = attend(query_rows, key_rows, VSEQ)
        mixed = mix_heads(attention, value_rows, VSEQ)
        target_blocks = target_rows.reshape(mixed.shape).astype(jnp.float32)
        val_residual = (mixed - target_blocks) / VSEQ
        pulled = jnp.einsum('grqk,qgrh->kgh', attention.astype(jnp.float32), val_residual, precision=lax.Precision.HIGHEST)
        return pulled.reshape(VSEQ, head_width)
    val_pull = lax.map(val_sequence, (val_q.reshape(VAL_SEQS, VSEQ, -1), val_k.reshape(VAL_SEQS, VSEQ, -1), val_values.reshape(VAL_SEQS, VSEQ, -1), val_target.reshape(VAL_SEQS, VSEQ, -1))).reshape(VAL_TOKENS, head_width)
    stacked = jnp.transpose(skill_grads, (1, 0, 2)).reshape(D, SKILLS * head_width)
    tangent = jnp.dot(val_x, stacked, preferred_element_type=jnp.float32).reshape(VAL_TOKENS, SKILLS, head_width)
    along = jnp.einsum('tsc,tc->ts', tangent, val_pull, precision=lax.Precision.HIGHEST)
    token_skill = jnp.repeat(val_skill, VSEQ)
    indicator = (token_skill[:, None] == jnp.arange(SKILLS, dtype=jnp.int32)[None, :]).astype(jnp.float32)
    transfer = step_size * jnp.dot(along.T, indicator, precision=lax.Precision.HIGHEST)
    return (skill_grads, transfer)
```

```python
import math

import jax
import jax.numpy as jnp
from jax import lax
from jax.sharding import PartitionSpec as P

HD = 128
SKILLS = 4
SEQ = 256
VSEQ = 128
NZ, NY, NC = 8, 2, 2
NX, NL = 4, 2

step_size = 0.01
bf16 = jnp.bfloat16
f32 = jnp.float32


def place(z, y, c):
    return (z % NZ) * 4 + (y % NY) * 2 + (c % NC)


def moves(fn):
    return [
        (place(z, y, c), place(*fn(z, y, c)))
        for z in range(NZ)
        for y in range(NY)
        for c in range(NC)
    ]


CORE = moves(lambda z, y, c: (z, y, c + 1))
YHI = moves(lambda z, y, c: (z, y + 1, c))
UP = moves(lambda z, y, c: (z + 1, y, c))
DOWN = moves(lambda z, y, c: (z - 1, y, c))


def send(value, way):
    return lax.ppermute(value, "fsdp", way)


def coords():
    f = lax.axis_index("fsdp")
    return f // 4, (f // 2) % 2, f % 2


def gather_fsdp(block):
    z, y, c = coords()
    other = send(block, YHI)
    pair = jnp.where(y == 0, jnp.stack([block, other]), jnp.stack([other, block]))
    up1, down1 = send(pair, UP), send(pair, DOWN)
    up2, down2 = send(up1, UP), send(down1, DOWN)
    up3, down3 = send(up2, UP), send(down2, DOWN)
    up4, down4 = send(up3[0], UP), send(down3[1], DOWN)
    far = jnp.stack([up4, down4])
    ring = jnp.stack([pair, down1, down2, down3, far, up3, up2, up1])
    ring = jnp.roll(ring, z, axis=0)
    swapped = send(ring, CORE)
    return jnp.where(c == 0, jnp.stack([ring, swapped], 2), jnp.stack([swapped, ring], 2))


def reduce_scatter_fsdp(terms):
    z, y, c = coords()
    mine = lax.dynamic_index_in_dim(terms, c, 2, keepdims=False)
    theirs = lax.dynamic_index_in_dim(terms, 1 - c, 2, keepdims=False).astype(bf16)
    chip = mine + send(theirs, CORE).astype(f32)

    def at(dz):
        return lax.dynamic_index_in_dim(chip, (z + dz) % NZ, 0, keepdims=False)

    far = at(4).astype(bf16)
    up, down = send(far[0], UP), send(far[1], DOWN)
    a, b = at(3), at(5)
    up = send(jnp.stack([a[0] + up.astype(f32), a[1]]).astype(bf16), UP)
    down = send(jnp.stack([b[0], b[1] + down.astype(f32)]).astype(bf16), DOWN)
    up = send((at(2) + up.astype(f32)).astype(bf16), UP)
    down = send((at(6) + down.astype(f32)).astype(bf16), DOWN)
    up = send((at(1) + up.astype(f32)).astype(bf16), UP)
    down = send((at(7) + down.astype(f32)).astype(bf16), DOWN)
    total = at(0) + up.astype(f32) + down.astype(f32)
    keep = lax.dynamic_index_in_dim(total, y, 0, keepdims=False)
    give = lax.dynamic_index_in_dim(total, 1 - y, 0, keepdims=False).astype(bf16)
    return keep + send(give, YHI).astype(f32)


def spread(value, way):
    return value + lax.ppermute(value, ("fsdp", "tp"), way)


def sum_all(value):
    value = value + send(value, CORE)
    for shifts in ((1, 2, 3), (4,)):
        got = [send(value, moves(lambda z, y, c, s=s: ((z // 4 * 4 + (z + s) % 4) if s < 4 else z + 4, y, c))) for s in shifts]
        value = value + sum(got)
    value = value + send(value, YHI)
    x_moves = [[(l * NX + x, l * NX + (x + s) % NX) for l in range(NL) for x in range(NX)] for s in (1, 2, 3)]
    value = value + sum(lax.ppermute(value, "tp", way) for way in x_moves)
    return value + lax.ppermute(value, "tp", [(i, (i + NX) % (NX * NL)) for i in range(NX * NL)])


def attend(query_rows, key_rows, length):
    members = query_rows.shape[0] // length
    kv_heads = key_rows.shape[1] // HD
    group = query_rows.shape[1] // HD // kv_heads
    queries = query_rows.reshape(members, length, kv_heads, group, HD)
    keys = key_rows.reshape(members, length, kv_heads, HD)
    scores = jnp.einsum("bqgrh,bkgh->bgrqk", queries, keys, preferred_element_type=f32) * (
        1.0 / math.sqrt(HD)
    )
    places = jnp.arange(length)
    allowed = places[:, None] >= places[None, :]
    scores = jnp.where(allowed, scores, jnp.float32(-1e30))
    highest = jnp.max(scores, axis=-1, keepdims=True)
    raised = jnp.exp(scores - highest)
    return (raised / jnp.sum(raised, axis=-1, keepdims=True)).astype(bf16)


def on_device(
    train_x, train_q, train_k, train_target, train_skill, value_weight, val_x, val_q, val_k, val_target, val_skill
):
    head_width = train_k.shape[1]
    kv_heads = head_width // HD
    group = train_q.shape[1] // head_width
    train_rows, val_rows = train_x.shape[0], val_x.shape[0]
    train_members = train_rows // SEQ
    skill_ids = jnp.arange(SKILLS, dtype=jnp.int32)
    f, t = lax.axis_index("fsdp"), lax.axis_index("tp")

    part = val_rows // 8
    own_tokens = lax.dynamic_slice_in_dim(val_x, t * part, part).reshape(part, 32, 256)
    crossed = lax.all_to_all(own_tokens.transpose(1, 0, 2), "fsdp", 0, 0)
    val_columns = lax.all_to_all(jnp.broadcast_to(crossed, (8,) + crossed.shape), "tp", 0, 0)

    weight = gather_fsdp(value_weight).reshape(-1, head_width)
    values = jnp.dot(train_x, weight, preferred_element_type=f32).astype(bf16)
    val_values = jnp.dot(val_x, weight, preferred_element_type=f32).astype(bf16)
    attention = attend(train_q, train_k, SEQ)
    value_blocks = values.reshape(train_members, SEQ, kv_heads, HD)
    mixed = jnp.einsum("bgrqk,bkgh->bqgrh", attention, value_blocks, preferred_element_type=f32)
    target_blocks = train_target.reshape(train_members, SEQ, kv_heads, group, HD).astype(f32)
    residual = ((mixed - target_blocks) / SEQ).astype(bf16)
    value_grads = jnp.einsum("bgrqk,bqgrh->bkgh", attention, residual, preferred_element_type=f32)
    grad_rows = value_grads.reshape(train_rows, head_width).astype(bf16)
    local_skill = lax.dynamic_slice_in_dim(train_skill, f * train_members, train_members)
    member = (jnp.repeat(local_skill, SEQ)[:, None] == skill_ids[None, :]).astype(bf16)
    masked = (grad_rows[:, None, :] * member[:, :, None]).reshape(train_rows, SKILLS * head_width)
    terms = lax.dot_general(train_x, masked, (((0,), (0,)), ((), ())), preferred_element_type=f32)
    sums = reduce_scatter_fsdp(terms.reshape(NZ, NY, NC, -1, SKILLS * head_width))
    skill_grads = sums.reshape(-1, SKILLS, head_width).transpose(1, 0, 2).astype(bf16)

    val_attention = attend(val_q, val_k, VSEQ)
    val_blocks = val_values.reshape(1, VSEQ, kv_heads, HD)
    val_mixed = jnp.einsum("bgrqk,bkgh->bqgrh", val_attention, val_blocks, preferred_element_type=f32)
    val_target_blocks = val_target.reshape(1, VSEQ, kv_heads, group, HD).astype(f32)
    val_residual = (val_mixed - val_target_blocks) / VSEQ
    val_pull = jnp.einsum(
        "bgrqk,bqgrh->bkgh", val_attention.astype(f32), val_residual, precision=lax.Precision.HIGHEST
    ).reshape(val_rows, head_width)
    pulls = gather_fsdp(val_pull.astype(bf16)).reshape(32, 8, part, head_width)
    val_member = (val_skill[:, None] == skill_ids[None, :]).astype(bf16)
    masked_pulls = pulls[:, :, :, None, :] * val_member[:, None, None, :, None]
    directions = jnp.einsum("tfid,ftivc->vdc", val_columns, masked_pulls, preferred_element_type=f32)
    local = jnp.einsum(
        "sdc,vdc->sv", skill_grads.astype(f32), directions, precision=lax.Precision.HIGHEST
    )
    transfer = sum_all(step_size * local)
    return (skill_grads, transfer)


def solution(mesh):
    placed = (
        P("fsdp", None),
        P("fsdp", "tp"),
        P("fsdp", "tp"),
        P("fsdp", "tp"),
        P(),
        P("fsdp", "tp"),
        P("fsdp", None),
        P("fsdp", "tp"),
        P("fsdp", "tp"),
        P("fsdp", "tp"),
        P(),
    )
    return jax.shard_map(
        on_device,
        mesh=mesh,
        in_specs=placed,
        out_specs=(P(None, "fsdp", "tp"), P()),
        check_vma=False,
    )
```

```python
import functools
import math

import jax
import jax.numpy as jnp
from jax import lax
from jax.experimental import pallas as pl
from jax.experimental.pallas import tpu as pltpu
from jax.sharding import PartitionSpec as P

HD = 128
GROUP = 8
SKILLS = 4
SEQ = 256
VSEQ = 128
MEMBERS = 4
NZ, NY, NC = 8, 2, 2
NX, NL = 4, 2
ROWS = 256

step_size = 0.01
bf16 = jnp.bfloat16
f32 = jnp.float32


def place(z, y, c):
    return (z % NZ) * 4 + (y % NY) * 2 + (c % NC)


def moves(fn):
    return [
        (place(z, y, c), place(*fn(z, y, c)))
        for z in range(NZ)
        for y in range(NY)
        for c in range(NC)
    ]


CORE = moves(lambda z, y, c: (z, y, c + 1))
YHI = moves(lambda z, y, c: (z, y + 1, c))
UP = moves(lambda z, y, c: (z + 1, y, c))
DOWN = moves(lambda z, y, c: (z - 1, y, c))


def send(value, way):
    return lax.ppermute(value, "fsdp", way)


def block_of(place_ref, dz, dy, dc):
    z, y, c = place_ref[0], place_ref[1], place_ref[2]
    return lax.rem(z + dz, NZ) * 4 + lax.rem(y + dy, NY) * 2 + lax.rem(c + dc, NC)


def vmem(shape):
    return pl.BlockSpec(shape, lambda i, *_: (0,) * len(shape))


def params(mib=56):
    return pltpu.CompilerParams(vmem_limit_bytes=mib * 2**20)


def cost(flops, moved, exps=0):
    return pl.CostEstimate(flops=flops, bytes_accessed=moved, transcendentals=exps)


def dot(a, b, dims=((1,), (0,))):
    return lax.dot_general(a, b, (dims, ((), ())), preferred_element_type=f32)


def attend_kernel(length, q_ref, k_ref, p_ref):
    keys = k_ref[...]
    rows = lax.broadcasted_iota(jnp.int32, (length, length), 0)
    columns = lax.broadcasted_iota(jnp.int32, (length, length), 1)
    allowed = rows >= columns
    for h in range(GROUP):
        scores = dot(q_ref[:, h * HD : (h + 1) * HD], keys, ((1,), (1,)))
        scores = jnp.where(allowed, scores * (1.0 / math.sqrt(HD)), jnp.float32(-1e30))
        raised = jnp.exp(scores - jnp.max(scores, axis=-1, keepdims=True))
        total = jnp.sum(raised, axis=-1, keepdims=True)
        p_ref[0, h] = (raised * (1.0 / total)).astype(bf16)


def attend(queries, keys, length):
    members = queries.shape[0] // length
    count = members * GROUP * length * length
    return pl.pallas_call(
        functools.partial(attend_kernel, length),
        grid=(members,),
        in_specs=[
            pl.BlockSpec((length, GROUP * HD), lambda i: (i, 0)),
            pl.BlockSpec((length, HD), lambda i: (i, 0)),
        ],
        out_specs=pl.BlockSpec((1, GROUP, length, length), lambda i: (i, 0, 0, 0)),
        out_shape=jax.ShapeDtypeStruct((members, GROUP, length, length), bf16),
        compiler_params=params(),
        cost_estimate=cost(2 * count * HD, 4 * count, count),
    )(queries, keys)


def x_specs(offsets):
    train = [
        pl.BlockSpec((SEQ, ROWS), lambda i, p, o=o: (i, block_of(p, *o))) for o in offsets
    ]
    val = [
        pl.BlockSpec((VSEQ, ROWS), lambda i, p, o=o: (0, block_of(p, *o))) for o in offsets
    ]
    return train, val


def offsets_of(zs):
    return [(dz, dy, dc) for dz in zs for dc in range(NC) for dy in range(NY)]


def project_kernel(n, first, place_ref, *refs):
    xs, refs = refs[:n], refs[n:]
    vs, refs = refs[:n], refs[n:]
    ws, refs = refs[: n // 2], refs[n // 2 :]
    (sum_in, val_in, sum_out, val_out) = (None, None, *refs) if first else refs
    total = sum(dot(xs[j][...], ws[j // 2][j % 2]) for j in range(n))
    sum_out[...] = total if first else total + sum_in[...]

    @pl.when(pl.program_id(0) == 0)
    def _():
        total = sum(dot(vs[j][...], ws[j // 2][j % 2]) for j in range(n))
        val_out[...] = total if first else total + val_in[...]


def project(where, train_x, val_x, zs, weights, sums):
    offsets = offsets_of(zs)
    n = len(offsets)
    train, val = x_specs(offsets)
    rows = train_x.shape[0]
    sum_specs = [pl.BlockSpec((SEQ, HD), lambda i, p: (i, 0)), vmem((VSEQ, HD))]
    first = sums is None
    return pl.pallas_call(
        functools.partial(project_kernel, n, first),
        grid_spec=pltpu.PrefetchScalarGridSpec(
            num_scalar_prefetch=1,
            grid=(MEMBERS,),
            in_specs=train + val + [vmem((NY, ROWS, HD))] * (n // 2) + ([] if first else sum_specs),
            out_specs=sum_specs,
        ),
        out_shape=[jax.ShapeDtypeStruct((rows, HD), f32), jax.ShapeDtypeStruct((VSEQ, HD), f32)],
        compiler_params=params(),
        cost_estimate=cost(4 * rows * n * ROWS * HD, 2 * rows * n * ROWS),
    )(where, *[train_x] * n, *[val_x] * n, *weights, *([] if first else sums))


def grads_kernel(n, place_ref, *refs):
    xs, refs = refs[:n], refs[n:]
    ws, (sum_ref, p_ref, target_ref, out_ref) = refs[: n // 2], refs[n // 2 :]
    total = sum_ref[...]
    for j in range(n):
        total += dot(xs[j][...], ws[j // 2][j % 2])
    values = total.astype(bf16)
    pulled = jnp.zeros((HD, SEQ), f32)
    for h in range(GROUP):
        attention = p_ref[0, h]
        mixed = dot(attention, values)
        target = target_ref[:, h * HD : (h + 1) * HD].astype(f32)
        residual = ((mixed - target) * (1.0 / SEQ)).astype(bf16)
        pulled += dot(residual, attention, ((0,), (0,)))
    out_ref[...] = pulled.astype(bf16)


def value_grads(where, train_x, zs, weights, sums, attention, target):
    offsets = offsets_of(zs)
    n = len(offsets)
    rows = train_x.shape[0]
    return pl.pallas_call(
        functools.partial(grads_kernel, n),
        grid_spec=pltpu.PrefetchScalarGridSpec(
            num_scalar_prefetch=1,
            grid=(MEMBERS,),
            in_specs=x_specs(offsets)[0]
            + [vmem((NY, ROWS, HD))] * (n // 2)
            + [
                pl.BlockSpec((SEQ, HD), lambda i, p: (i, 0)),
                pl.BlockSpec((1, GROUP, SEQ, SEQ), lambda i, p: (i, 0, 0, 0)),
                pl.BlockSpec((SEQ, GROUP * HD), lambda i, p: (i, 0)),
            ],
            out_specs=pl.BlockSpec((HD, SEQ), lambda i, p: (0, i)),
        ),
        out_shape=jax.ShapeDtypeStruct((HD, rows), bf16),
        compiler_params=params(),
        cost_estimate=cost(4 * rows * GROUP * SEQ * HD, 8 * 2**20),
    )(where, *[train_x] * n, *weights, sums, attention, target)


def val_kernel(n, place_ref, *refs):
    vs, refs = refs[:n], refs[n:]
    ws, (sum_ref, p_ref, target_ref, out_ref) = refs[: n // 2], refs[n // 2 :]
    total = sum_ref[...]
    for j in range(n):
        total += dot(vs[j][...], ws[j // 2][j % 2])
    values = total.astype(bf16)
    pulled = jnp.zeros((HD, VSEQ), f32)
    for h in range(GROUP):
        attention = p_ref[0, h]
        target = target_ref[:, h * HD : (h + 1) * HD].astype(f32)
        residual = (dot(attention, values) - target) * (1.0 / VSEQ)
        high = residual.astype(bf16)
        low = (residual - high.astype(f32)).astype(bf16)
        pulled += dot(high, attention, ((0,), (0,))) + dot(low, attention, ((0,), (0,)))
    out_ref[...] = pulled.astype(bf16)


def val_pulls(where, val_x, zs, weights, sums, attention, target):
    offsets = offsets_of(zs)
    n = len(offsets)
    return pl.pallas_call(
        functools.partial(val_kernel, n),
        grid_spec=pltpu.PrefetchScalarGridSpec(
            num_scalar_prefetch=1,
            grid=(1,),
            in_specs=x_specs(offsets)[1]
            + [vmem((NY, ROWS, HD))] * (n // 2)
            + [vmem((VSEQ, HD)), vmem((1, GROUP, VSEQ, VSEQ)), vmem((VSEQ, GROUP * HD))],
            out_specs=vmem((HD, VSEQ)),
        ),
        out_shape=jax.ShapeDtypeStruct((HD, VSEQ), bf16),
        compiler_params=params(),
        cost_estimate=cost(10 * VSEQ * GROUP * VSEQ * HD, 2**20),
    )(where, *[val_x] * n, *weights, sums, attention, target)


def skills_kernel(place_ref, theirs_x, mine_x, grads_ref, theirs_ref, mine_ref, total):
    for x_ref, out_ref in ((theirs_x, theirs_ref), (mine_x, mine_ref)):
        total[...] = jnp.zeros_like(total)
        for m in range(MEMBERS):
            product = dot(grads_ref[:, m * SEQ : (m + 1) * SEQ], x_ref[m * SEQ : (m + 1) * SEQ, :])
            total[place_ref[3 + m]] += product
        out_ref[0, 0] = total[...].reshape(SKILLS * HD, ROWS).astype(out_ref.dtype)


def skill_terms(where, train_x, grads, zs):
    rows = train_x.shape[0]
    table = jnp.array(zs, jnp.int32)

    def x_at(dc):
        return pl.BlockSpec(
            (rows, ROWS),
            lambda i, j, p, t: (0, block_of(p, t[i], j, dc)),
        )

    out = pl.BlockSpec((1, 1, SKILLS * HD, ROWS), lambda i, j, p, t: (i, j, 0, 0))
    shape = (len(zs), NY, SKILLS * HD, ROWS)
    return pl.pallas_call(
        lambda p, t, *refs: skills_kernel(p, *refs),
        grid_spec=pltpu.PrefetchScalarGridSpec(
            num_scalar_prefetch=2,
            grid=(len(zs), NY),
            in_specs=[x_at(1), x_at(0), pl.BlockSpec((HD, rows), lambda i, j, p, t: (0, 0))],
            out_specs=[out, out],
            scratch_shapes=[pltpu.VMEM((SKILLS, HD, ROWS), f32)],
        ),
        out_shape=[jax.ShapeDtypeStruct(shape, bf16), jax.ShapeDtypeStruct(shape, f32)],
        compiler_params=params(),
        cost_estimate=cost(8 * rows * len(zs) * NY * ROWS * HD, len(zs) * 5 * 2**20),
    )(where, table, train_x, train_x, grads)


def directions_kernel(skill_ref, pulls_ref, x_ref, out_ref):
    out_ref[...] = jnp.zeros_like(out_ref)
    for f in range(NZ * NY * NC):
        tokens = x_ref[:, f].reshape(VSEQ, ROWS)
        out_ref[skill_ref[f]] += dot(pulls_ref[f], tokens)


def directions_of(val_skill, pulls, columns):
    return pl.pallas_call(
        directions_kernel,
        grid_spec=pltpu.PrefetchScalarGridSpec(
            num_scalar_prefetch=1,
            grid=(1,),
            in_specs=[vmem(pulls.shape), vmem(columns.shape)],
            out_specs=vmem((SKILLS, HD, ROWS)),
        ),
        out_shape=jax.ShapeDtypeStruct((SKILLS, HD, ROWS), f32),
        compiler_params=params(),
        cost_estimate=cost(2 * 4096 * ROWS * HD, 4 * 2**20),
    )(val_skill, pulls, columns)


def finish_kernel(keep_ref, got_ref, directions_ref, grads_ref, local_ref):
    pieces = []
    for s in range(SKILLS):
        rows = slice(s * HD, (s + 1) * HD)
        total = keep_ref[rows, :] + got_ref[rows, :].astype(f32)
        rounded = total.astype(bf16).astype(f32)
        grads_ref[s] = rounded.T.astype(bf16)
        for v in range(SKILLS):
            pieces.append(jnp.sum(rounded * directions_ref[v], axis=0, keepdims=True))
    sums = step_size * jnp.sum(jnp.concatenate(pieces, axis=0), axis=1, keepdims=True)
    local_ref[...] = jnp.broadcast_to(sums, local_ref.shape)


def finish(keep, got, directions):
    return pl.pallas_call(
        finish_kernel,
        out_shape=[
            jax.ShapeDtypeStruct((SKILLS, ROWS, HD), bf16),
            jax.ShapeDtypeStruct((SKILLS * SKILLS, HD), f32),
        ],
        compiler_params=params(),
        cost_estimate=cost(2**20, 2**20),
    )(keep, got, directions)


def ring_gather(block, extra=lambda dz: None):
    pair = jnp.stack([block, send(block, YHI)])
    blocks = {0: pair}
    up, down = pair, pair
    for step in (1, 2, 3):
        up, down = send(up, UP), send(down, DOWN)
        blocks[NZ - step], blocks[step] = up, down
    blocks[4] = jnp.stack([send(up[0], UP), send(down[1], DOWN)])
    return blocks


def sum_all(value):
    value = value + send(value, CORE)
    for shifts in ((1, 2, 3), (4,)):
        got = [send(value, moves(lambda z, y, c, s=s: ((z // 4 * 4 + (z + s) % 4) if s < 4 else z + 4, y, c))) for s in shifts]
        value = value + sum(got)
    value = value + send(value, YHI)
    x_moves = [[(l * NX + x, l * NX + (x + s) % NX) for l in range(NL) for x in range(NX)] for s in (1, 2, 3)]
    value = value + sum(lax.ppermute(value, "tp", way) for way in x_moves)
    return value + lax.ppermute(value, "tp", [(i, (i + NX) % (NX * NL)) for i in range(NX * NL)])


def on_device(
    train_x, train_q, train_k, train_target, train_skill, value_weight, val_x, val_q, val_k, val_target, val_skill
):
    f, t = lax.axis_index("fsdp"), lax.axis_index("tp")
    z, y, c = f // 4, (f // 2) % 2, f % 2
    own_skill = lax.dynamic_slice_in_dim(train_skill, f * MEMBERS, MEMBERS)
    where = jnp.concatenate([jnp.stack([z, y, c]).astype(jnp.int32), own_skill])

    part = VSEQ // 8
    own_tokens = lax.dynamic_slice_in_dim(val_x, t * part, part).reshape(part, 32, ROWS)
    crossed = lax.all_to_all(own_tokens.transpose(1, 0, 2), "fsdp", 0, 0)
    val_columns = lax.all_to_all(jnp.broadcast_to(crossed, (8,) + crossed.shape), "tp", 0, 0)

    near = ring_gather(value_weight)
    weights = {dz: [near[dz], send(near[dz], CORE)] for dz in range(NZ)}
    attention = attend(train_q, train_k, SEQ)
    val_attention = attend(val_q, val_k, VSEQ)
    sums = project(where, train_x, val_x, (0,), weights[0], None)
    for dz in (1, 2, 3):
        sums = project(where, train_x, val_x, (dz, NZ - dz), weights[dz] + weights[NZ - dz], sums)
    grads = value_grads(where, train_x, (4,), weights[4], sums[0], attention, train_target)
    pull = val_pulls(where, val_x, (4,), weights[4], sums[1], val_attention, val_target)

    chip = {}
    for zs in ((4,), (3, 5), (2, 6), (1, 7), (0,)):
        theirs, mine = skill_terms(where, train_x, grads, zs)
        total = mine + send(theirs, CORE).astype(f32)
        for i, dz in enumerate(zs):
            chip[dz] = total[i]
    far = chip[4].astype(bf16)
    up, down = send(far[0], UP), send(far[1], DOWN)
    a, b = chip[3], chip[5]
    up = send(jnp.stack([a[0] + up.astype(f32), a[1]]).astype(bf16), UP)
    down = send(jnp.stack([b[0], b[1] + down.astype(f32)]).astype(bf16), DOWN)
    for dz in (2, 1):
        up = send((chip[dz] + up.astype(f32)).astype(bf16), UP)
        down = send((chip[NZ - dz] + down.astype(f32)).astype(bf16), DOWN)
    total = chip[0] + up.astype(f32) + down.astype(f32)
    got = send(total[1].astype(bf16), YHI)

    near_pulls = ring_gather(pull)
    pulls = jnp.stack([near_pulls[dz] for dz in range(NZ)])
    pulls = jnp.roll(jnp.where(y == 0, pulls, pulls[:, ::-1]), z, axis=0)
    swapped = send(pulls, CORE)
    pulls = jnp.where(c == 0, jnp.stack([pulls, swapped], 2), jnp.stack([swapped, pulls], 2))
    directions = directions_of(val_skill, pulls.reshape(32, HD, VSEQ), val_columns)
    skill_grads, local = finish(total[0], got, directions)
    transfer = sum_all(local[:, 0].reshape(SKILLS, SKILLS))
    return (skill_grads, transfer)


def solution(mesh):
    placed = (
        P("fsdp", None),
        P("fsdp", "tp"),
        P("fsdp", "tp"),
        P("fsdp", "tp"),
        P(),
        P("fsdp", "tp"),
        P("fsdp", None),
        P("fsdp", "tp"),
        P("fsdp", "tp"),
        P("fsdp", "tp"),
        P(),
    )
    return jax.shard_map(
        on_device,
        mesh=mesh,
        in_specs=placed,
        out_specs=(P(None, "fsdp", "tp"), P()),
        check_vma=False,
    )
```

```python
import functools
import math

import jax
import jax.numpy as jnp
from jax import lax
from jax.experimental import pallas as pl
from jax.experimental.pallas import tpu as pltpu
from jax.sharding import PartitionSpec as P

HD = 128
GROUP = 8
SKILLS = 4
SEQ = 256
VSEQ = 128
MEMBERS = 4
NZ, NY, NC = 8, 2, 2
NX, NL = 4, 2
ROWS = 256

step_size = 0.01
bf16 = jnp.bfloat16
f32 = jnp.float32


def place(z, y, c):
    return (z % NZ) * 4 + (y % NY) * 2 + (c % NC)


def moves(fn):
    return [
        (place(z, y, c), place(*fn(z, y, c)))
        for z in range(NZ)
        for y in range(NY)
        for c in range(NC)
    ]


CORE = moves(lambda z, y, c: (z, y, c + 1))
YHI = moves(lambda z, y, c: (z, y + 1, c))
UP = moves(lambda z, y, c: (z + 1, y, c))
DOWN = moves(lambda z, y, c: (z - 1, y, c))


def send(value, way):
    return lax.ppermute(value, "fsdp", way)


def after(value, *others):
    return lax.optimization_barrier((value, *others))[0]


def vmem(shape):
    return pl.BlockSpec(shape, lambda i, *_: (0,) * len(shape))


def params(mib=56):
    return pltpu.CompilerParams(vmem_limit_bytes=mib * 2**20)


def cost(flops, moved, exps=0):
    return pl.CostEstimate(flops=flops, bytes_accessed=moved, transcendentals=exps)


def dot(a, b, dims=((1,), (0,))):
    return lax.dot_general(a, b, (dims, ((), ())), preferred_element_type=f32)


def attend_kernel(length, q_ref, k_ref, p_ref):
    keys = k_ref[...]
    rows = lax.broadcasted_iota(jnp.int32, (length, length), 0)
    columns = lax.broadcasted_iota(jnp.int32, (length, length), 1)
    allowed = rows >= columns
    for h in range(GROUP):
        scores = dot(q_ref[:, h * HD : (h + 1) * HD], keys, ((1,), (1,)))
        scores = jnp.where(allowed, scores * (1.0 / math.sqrt(HD)), jnp.float32(-1e30))
        raised = jnp.exp(scores - jnp.max(scores, axis=-1, keepdims=True))
        total = jnp.sum(raised, axis=-1, keepdims=True)
        p_ref[0, h] = (raised * (1.0 / total)).astype(bf16)


def attend(queries, keys, length):
    members = queries.shape[0] // length
    count = members * GROUP * length * length
    return pl.pallas_call(
        functools.partial(attend_kernel, length),
        grid=(members,),
        in_specs=[
            pl.BlockSpec((length, GROUP * HD), lambda i: (i, 0)),
            pl.BlockSpec((length, HD), lambda i: (i, 0)),
        ],
        out_specs=pl.BlockSpec((1, GROUP, length, length), lambda i: (i, 0, 0, 0)),
        out_shape=jax.ShapeDtypeStruct((members, GROUP, length, length), bf16),
        compiler_params=params(),
        cost_estimate=cost(2 * count * HD, 4 * count, count),
    )(queries, keys)


def z_of(place_ref, dz):
    return lax.rem(place_ref[0] + dz, NZ)


def lay_weights(place_ref, near_ref, far_ref, whole):
    for dc, ref in enumerate((near_ref, far_ref)):
        for dy in range(NY):
            y = lax.rem(place_ref[1] + dy, NY)
            c = lax.rem(place_ref[2] + dc, NC)
            row = pl.multiple_of((y * 2 + c) * ROWS, ROWS)
            whole[pl.ds(row, ROWS), :] = ref[dy]


def project_kernel(n, first, place_ref, *refs):
    xs, refs = refs[:n], refs[n:]
    vs, refs = refs[:n], refs[n:]
    ws, refs = refs[: 2 * n], refs[2 * n :]
    if first:
        sum_out, val_out, *whole = refs
    else:
        sum_in, val_in, sum_out, val_out, *whole = refs

    @pl.when(pl.program_id(0) == 0)
    def _():
        for j in range(n):
            lay_weights(place_ref, ws[2 * j], ws[2 * j + 1], whole[j])
        total = sum(dot(vs[j][...], whole[j][...]) for j in range(n))
        val_out[...] = total if first else total + val_in[...]

    total = sum(dot(xs[j][...], whole[j][...]) for j in range(n))
    sum_out[...] = total if first else total + sum_in[...]


WIDE = NY * NC * ROWS
TILE = 512


def project(where, train_x, val_x, zs, weights, sums):
    n = len(zs)
    rows = train_x.shape[0]
    sum_specs = [pl.BlockSpec((TILE, HD), lambda i, p: (i, 0)), vmem((VSEQ, HD))]
    first = sums is None
    return pl.pallas_call(
        functools.partial(project_kernel, n, first),
        grid_spec=pltpu.PrefetchScalarGridSpec(
            num_scalar_prefetch=1,
            grid=(rows // TILE,),
            in_specs=[pl.BlockSpec((TILE, WIDE), lambda i, p, dz=dz: (i, z_of(p, dz))) for dz in zs]
            + [pl.BlockSpec((VSEQ, WIDE), lambda i, p, dz=dz: (0, z_of(p, dz))) for dz in zs]
            + [vmem((NY, ROWS, HD))] * (2 * n)
            + ([] if first else sum_specs),
            out_specs=sum_specs,
            scratch_shapes=[pltpu.VMEM((WIDE, HD), bf16)] * n,
        ),
        out_shape=[jax.ShapeDtypeStruct((rows, HD), f32), jax.ShapeDtypeStruct((VSEQ, HD), f32)],
        compiler_params=params(),
        cost_estimate=cost(2 * rows * n * WIDE * HD, 2 * rows * n * WIDE),
    )(where, *[train_x] * n, *[val_x] * n, *weights, *([] if first else sums))


def grads_kernel(place_ref, x_ref, near_ref, far_ref, sum_ref, p_ref, target_ref, out_ref, whole):
    @pl.when(pl.program_id(0) == 0)
    def _():
        lay_weights(place_ref, near_ref, far_ref, whole)

    values = (sum_ref[...] + dot(x_ref[...], whole[...])).astype(bf16)
    attention = p_ref[0].reshape(GROUP * SEQ, SEQ)
    mixed = dot(attention, values)
    target = jnp.concatenate(
        [target_ref[:, h * HD : (h + 1) * HD] for h in range(GROUP)], axis=0
    ).astype(f32)
    residual = ((mixed - target) * (1.0 / SEQ)).astype(bf16)
    pulled = dot(residual, attention, ((0,), (0,)))
    skill = place_ref[3 + pl.program_id(0)]
    for s in range(SKILLS):
        out_ref[s * HD : (s + 1) * HD, :] = (pulled * (skill == s).astype(f32)).astype(bf16)


def value_grads(where, train_x, weights, sums, attention, target):
    rows = train_x.shape[0]
    return pl.pallas_call(
        grads_kernel,
        grid_spec=pltpu.PrefetchScalarGridSpec(
            num_scalar_prefetch=1,
            grid=(MEMBERS,),
            in_specs=[
                pl.BlockSpec((SEQ, WIDE), lambda i, p: (i, z_of(p, 4))),
                vmem((NY, ROWS, HD)),
                vmem((NY, ROWS, HD)),
                pl.BlockSpec((SEQ, HD), lambda i, p: (i, 0)),
                pl.BlockSpec((1, GROUP, SEQ, SEQ), lambda i, p: (i, 0, 0, 0)),
                pl.BlockSpec((SEQ, GROUP * HD), lambda i, p: (i, 0)),
            ],
            out_specs=pl.BlockSpec((SKILLS * HD, SEQ), lambda i, p: (0, i)),
            scratch_shapes=[pltpu.VMEM((WIDE, HD), bf16)],
        ),
        out_shape=jax.ShapeDtypeStruct((SKILLS * HD, rows), bf16),
        compiler_params=params(),
        cost_estimate=cost(4 * rows * GROUP * SEQ * HD, 8 * 2**20),
    )(where, train_x, *weights, sums, attention, target)


def val_kernel(place_ref, x_ref, near_ref, far_ref, sum_ref, p_ref, target_ref, out_ref, whole):
    lay_weights(place_ref, near_ref, far_ref, whole)
    values = (sum_ref[...] + dot(x_ref[...], whole[...])).astype(bf16)
    attention = p_ref[0].reshape(GROUP * VSEQ, VSEQ)
    target = jnp.concatenate(
        [target_ref[:, h * HD : (h + 1) * HD] for h in range(GROUP)], axis=0
    ).astype(f32)
    residual = (dot(attention, values) - target) * (1.0 / VSEQ)
    high = residual.astype(bf16)
    low = (residual - high.astype(f32)).astype(bf16)
    pulled = dot(high, attention, ((0,), (0,))) + dot(low, attention, ((0,), (0,)))
    out_ref[...] = pulled.astype(bf16)


def val_pulls(where, val_x, weights, sums, attention, target):
    return pl.pallas_call(
        val_kernel,
        grid_spec=pltpu.PrefetchScalarGridSpec(
            num_scalar_prefetch=1,
            grid=(1,),
            in_specs=[
                pl.BlockSpec((VSEQ, WIDE), lambda i, p: (0, z_of(p, 4))),
                vmem((NY, ROWS, HD)),
                vmem((NY, ROWS, HD)),
                vmem((VSEQ, HD)),
                vmem((1, GROUP, VSEQ, VSEQ)),
                vmem((VSEQ, GROUP * HD)),
            ],
            out_specs=vmem((HD, VSEQ)),
            scratch_shapes=[pltpu.VMEM((WIDE, HD), bf16)],
        ),
        out_shape=jax.ShapeDtypeStruct((HD, VSEQ), bf16),
        compiler_params=params(),
        cost_estimate=cost(10 * VSEQ * GROUP * VSEQ * HD, 2**20),
    )(where, val_x, *weights, sums, attention, target)


def skills_kernel(place_ref, x_ref, grads_ref, theirs_ref, mine_ref):
    for dc, out_ref in ((1, theirs_ref), (0, mine_ref)):
        column = pl.multiple_of(lax.rem(place_ref[2] + dc, NC) * ROWS, ROWS)
        out_ref[0, 0] = dot(grads_ref[...], x_ref[:, pl.ds(column, ROWS)]).astype(out_ref.dtype)


def skill_terms(where, train_x, grads, zs):
    rows = train_x.shape[0]
    first, step = zs[0], zs[-1] - zs[0]
    out = pl.BlockSpec((1, 1, SKILLS * HD, ROWS), lambda i, j, p: (i, j, 0, 0))
    shape = (len(zs), NY, SKILLS * HD, ROWS)
    return pl.pallas_call(
        skills_kernel,
        grid_spec=pltpu.PrefetchScalarGridSpec(
            num_scalar_prefetch=1,
            grid=(len(zs), NY),
            in_specs=[
                pl.BlockSpec(
                    (rows, NC * ROWS),
                    lambda i, j, p: (0, z_of(p, first + i * step) * 2 + lax.rem(p[1] + j, NY)),
                ),
                pl.BlockSpec((SKILLS * HD, rows), lambda i, j, p: (0, 0)),
            ],
            out_specs=[out, out],
        ),
        out_shape=[jax.ShapeDtypeStruct(shape, bf16), jax.ShapeDtypeStruct(shape, f32)],
        compiler_params=params(),
        cost_estimate=cost(2 * rows * len(zs) * WIDE * HD * SKILLS, len(zs) * 5 * 2**20),
    )(where, train_x, grads)


def directions_kernel(place_ref, skill_ref, near_ref, far_ref, x_ref, out_ref):
    out_ref[...] = jnp.zeros_like(out_ref)
    for dz in range(NZ):
        for dy in range(NY):
            for dc, ref in enumerate((near_ref, far_ref)):
                f = z_of(place_ref, dz) * 4 + lax.rem(place_ref[1] + dy, NY) * 2 + lax.rem(place_ref[2] + dc, NC)
                tokens = x_ref[:, f].reshape(VSEQ, ROWS)
                out_ref[skill_ref[f]] += dot(ref[dz, dy], tokens)


def directions_of(where, val_skill, near, far, columns):
    return pl.pallas_call(
        directions_kernel,
        grid_spec=pltpu.PrefetchScalarGridSpec(
            num_scalar_prefetch=2,
            grid=(1,),
            in_specs=[vmem(near.shape), vmem(far.shape), vmem(columns.shape)],
            out_specs=vmem((SKILLS, HD, ROWS)),
        ),
        out_shape=jax.ShapeDtypeStruct((SKILLS, HD, ROWS), f32),
        compiler_params=params(),
        cost_estimate=cost(2 * 4096 * ROWS * HD, 4 * 2**20),
    )(where, val_skill, near, far, columns)


def finish_kernel(keep_ref, got_ref, directions_ref, grads_ref, local_ref):
    lane = lax.broadcasted_iota(jnp.int32, (1, HD), 1)
    local = jnp.zeros((1, HD), f32)
    for s in range(SKILLS):
        rows = slice(s * HD, (s + 1) * HD)
        total = keep_ref[rows, :] + got_ref[rows, :].astype(f32)
        rounded = total.astype(bf16).astype(f32)
        grads_ref[s] = rounded.T.astype(bf16)
        for v in range(SKILLS):
            product = jnp.sum(rounded * directions_ref[v], axis=0, keepdims=True)
            entry = step_size * jnp.sum(product, axis=1, keepdims=True)
            local = jnp.where(lane == s * SKILLS + v, entry, local)
    local_ref[...] = local


def finish(keep, got, directions):
    return pl.pallas_call(
        finish_kernel,
        out_shape=[
            jax.ShapeDtypeStruct((SKILLS, ROWS, HD), bf16),
            jax.ShapeDtypeStruct((1, HD), f32),
        ],
        compiler_params=params(),
        cost_estimate=cost(2**20, 2**20),
    )(keep, got, directions)


def sum_all(row):
    copies = jnp.broadcast_to(row, (NZ * NY * NC * NX * NL,) + row.shape)
    return jnp.sum(lax.all_to_all(copies, ("fsdp", "tp"), 0, 0), axis=0)


def on_device(
    train_x, train_q, train_k, train_target, train_skill, value_weight, val_x, val_q, val_k, val_target, val_skill
):
    f, t = lax.axis_index("fsdp"), lax.axis_index("tp")
    z, y, c = f // 4, (f // 2) % 2, f % 2
    own_skill = lax.dynamic_slice_in_dim(train_skill, f * MEMBERS, MEMBERS)
    where = jnp.concatenate([jnp.stack([z, y, c]).astype(jnp.int32), own_skill])

    attention = attend(train_q, train_k, SEQ)
    val_attention = attend(val_q, val_k, VSEQ)
    pair = jnp.stack([value_weight, after(send(value_weight, YHI), val_attention)])

    def with_core(*blocks):
        return [w for block in blocks for w in (block, send(block, CORE))]

    up1, down1 = send(pair, UP), send(pair, DOWN)
    up1, down1 = after(up1, attention), after(down1, attention)
    sums = project(where, train_x, val_x, (0,), with_core(after(pair, attention)), None)
    part = VSEQ // 8
    own_tokens = lax.dynamic_slice_in_dim(after(val_x, up1), t * part, part).reshape(part, 32, ROWS)
    crossed = lax.all_to_all(own_tokens.transpose(1, 0, 2), "fsdp", 0, 0)
    up2, down2 = send(up1, UP), send(down1, DOWN)
    up2, down2 = after(up2, sums[0]), after(down2, sums[0])
    sums = project(where, train_x, val_x, (1, 7), with_core(down1, up1), sums)
    up3, down3 = send(up2, UP), send(down2, DOWN)
    up3, down3 = after(up3, sums[0]), after(down3, sums[0])
    sums = project(where, train_x, val_x, (2, 6), with_core(down2, up2), sums)
    far_pair = jnp.stack([send(up3[0], UP), after(send(down3[1], DOWN), sums[0])])
    sums = project(where, train_x, val_x, (3, 5), with_core(down3, up3), sums)
    last = with_core(far_pair)
    grads = value_grads(where, train_x, last, after(sums[0], crossed), attention, train_target)

    def terms(zs, *others):
        theirs, mine = skill_terms(where, train_x, after(grads, *others), zs)
        return mine + send(theirs, CORE).astype(f32), theirs

    chip = {}
    chip[4] = terms((4,))[0][0]
    far = chip[4].astype(bf16)
    up, down = send(far[0], UP), send(far[1], DOWN)
    both, theirs = terms((3, 5), far)
    chip[3], chip[5] = both[0], both[1]
    pull = val_pulls(where, val_x, last, after(sums[1], theirs), val_attention, val_target)
    pull = jnp.stack([pull, send(pull, YHI)])
    columns = lax.all_to_all(after(jnp.broadcast_to(crossed, (8,) + crossed.shape), pull), "tp", 0, 0)
    pulls = {0: pull}
    p_up, p_down = send(pull, UP), send(pull, DOWN)
    pulls[7], pulls[1] = p_up, p_down

    both, _ = terms((2, 6), up, down, pull)
    chip[2], chip[6] = both[0], both[1]
    a, b = chip[3], chip[5]
    up = send(jnp.stack([a[0] + up.astype(f32), a[1]]).astype(bf16), UP)
    down = send(jnp.stack([b[0], b[1] + down.astype(f32)]).astype(bf16), DOWN)

    both, _ = terms((1, 7), up, down)
    chip[1], chip[7] = both[0], both[1]
    p_up, p_down = send(after(p_up, up), UP), send(after(p_down, up), DOWN)
    pulls[6], pulls[2] = p_up, p_down
    up = send((chip[2] + up.astype(f32)).astype(bf16), UP)
    down = send((chip[6] + down.astype(f32)).astype(bf16), DOWN)

    both, _ = terms((0,), up, down)
    chip[0] = both[0]
    p_up, p_down = send(after(p_up, up), UP), send(after(p_down, up), DOWN)
    pulls[5], pulls[3] = p_up, p_down
    pulls[4] = jnp.stack([send(p_up[0], UP), send(p_down[1], DOWN)])
    up = send((chip[1] + up.astype(f32)).astype(bf16), UP)
    down = send((chip[7] + down.astype(f32)).astype(bf16), DOWN)

    near_pulls = jnp.stack([pulls[dz] for dz in range(NZ)])
    directions = directions_of(where, val_skill, near_pulls, send(near_pulls, CORE), columns)
    total = chip[0] + up.astype(f32) + down.astype(f32)
    got = send(total[1].astype(bf16), YHI)
    skill_grads, local = finish(total[0], got, directions)
    row = sum_all(local)
    return (skill_grads, row[0, : SKILLS * SKILLS].reshape(SKILLS, SKILLS))


def solution(mesh):
    placed = (
        P("fsdp", None),
        P("fsdp", "tp"),
        P("fsdp", "tp"),
        P("fsdp", "tp"),
        P(),
        P("fsdp", "tp"),
        P("fsdp", None),
        P("fsdp", "tp"),
        P("fsdp", "tp"),
        P("fsdp", "tp"),
        P(),
    )
    return jax.shard_map(
        on_device,
        mesh=mesh,
        in_specs=placed,
        out_specs=(P(None, "fsdp", "tp"), P()),
        check_vma=False,
    )
```

```python
import functools
import math

import jax
import jax.numpy as jnp
from jax import lax
from jax.experimental import pallas as pl
from jax.experimental.pallas import tpu as pltpu
from jax.sharding import PartitionSpec as P

HD = 128
GROUP = 8
SKILLS = 4
SEQ = 256
VSEQ = 128
MEMBERS = 4
NZ, NY, NC = 8, 2, 2
NX, NL = 4, 2
ROWS = 256

step_size = 0.01
bf16 = jnp.bfloat16
f32 = jnp.float32


def place(z, y, c):
    return (z % NZ) * 4 + (y % NY) * 2 + (c % NC)


def moves(fn):
    return [
        (place(z, y, c), place(*fn(z, y, c)))
        for z in range(NZ)
        for y in range(NY)
        for c in range(NC)
    ]


CORE = moves(lambda z, y, c: (z, y, c + 1))
YHI = moves(lambda z, y, c: (z, y + 1, c))
UP = moves(lambda z, y, c: (z + 1, y, c))
DOWN = moves(lambda z, y, c: (z - 1, y, c))


def send(value, way):
    return lax.ppermute(value, "fsdp", way)


def call(kernel, prefetched, operands, waits, grid, in_specs, out_specs, out_shape, cost_estimate, scratch=(), mib=50):
    first = len(prefetched) + len(operands)

    def body(*refs):
        kernel(*refs[:first], *refs[first + len(waits) :])

    return pl.pallas_call(
        body,
        grid_spec=pltpu.PrefetchScalarGridSpec(
            num_scalar_prefetch=len(prefetched),
            grid=grid,
            in_specs=list(in_specs) + [pl.BlockSpec(memory_space=pl.ANY)] * len(waits),
            out_specs=out_specs,
            scratch_shapes=list(scratch),
        ),
        out_shape=out_shape,
        compiler_params=pltpu.CompilerParams(vmem_limit_bytes=mib * 2**20),
        cost_estimate=cost_estimate,
    )(*prefetched, *operands, *waits)


def joined(values, waits):
    return pl.pallas_call(
        lambda *refs: None,
        in_specs=[pl.BlockSpec(memory_space=pl.ANY)] * (len(values) + len(waits)),
        out_specs=[pl.BlockSpec(memory_space=pl.ANY)] * len(values),
        out_shape=[jax.ShapeDtypeStruct(v.shape, v.dtype) for v in values],
        input_output_aliases={i: i for i in range(len(values))},
        compiler_params=pltpu.CompilerParams(vmem_limit_bytes=50 * 2**20),
        cost_estimate=cost(1, 1),
    )(*values, *waits)


def vmem(shape):
    return pl.BlockSpec(shape, lambda i, *_: (0,) * len(shape))


def cost(flops, moved, exps=0):
    return pl.CostEstimate(flops=flops // 64, bytes_accessed=moved // 64, transcendentals=exps // 64)


def dot(a, b, dims=((1,), (0,))):
    return lax.dot_general(a, b, (dims, ((), ())), preferred_element_type=f32)


def attend_kernel(length, q_ref, k_ref, p_ref):
    keys = k_ref[...]
    rows = lax.broadcasted_iota(jnp.int32, (length, length), 0)
    columns = lax.broadcasted_iota(jnp.int32, (length, length), 1)
    allowed = rows >= columns
    for h in range(GROUP):
        scores = dot(q_ref[:, h * HD : (h + 1) * HD], keys, ((1,), (1,)))
        scores = jnp.where(allowed, scores * (1.0 / math.sqrt(HD)), jnp.float32(-1e30))
        raised = jnp.exp(scores - jnp.max(scores, axis=-1, keepdims=True))
        total = jnp.sum(raised, axis=-1, keepdims=True)
        p_ref[0, h] = (raised * (1.0 / total)).astype(bf16)


def attend(queries, keys, length, waits=()):
    members = queries.shape[0] // length
    count = members * GROUP * length * length
    return call(
        functools.partial(attend_kernel, length),
        (),
        (queries, keys),
        waits,
        (members,),
        [
            pl.BlockSpec((length, GROUP * HD), lambda i: (i, 0)),
            pl.BlockSpec((length, HD), lambda i: (i, 0)),
        ],
        pl.BlockSpec((1, GROUP, length, length), lambda i: (i, 0, 0, 0)),
        jax.ShapeDtypeStruct((members, GROUP, length, length), bf16),
        cost(2 * count * HD, 4 * count, count),
    )


def z_of(place_ref, dz):
    return lax.rem(place_ref[0] + dz, NZ)


def lay_weights(place_ref, near_ref, far_ref, whole):
    for dc, ref in enumerate((near_ref, far_ref)):
        for dy in range(NY):
            y = lax.rem(place_ref[1] + dy, NY)
            c = lax.rem(place_ref[2] + dc, NC)
            row = pl.multiple_of((y * 2 + c) * ROWS, ROWS)
            whole[pl.ds(row, ROWS), :] = ref[dy]


def project_kernel(n, first, place_ref, *refs):
    xs, refs = refs[:n], refs[n:]
    vs, refs = refs[:n], refs[n:]
    ws, refs = refs[: 2 * n], refs[2 * n :]
    if first:
        sum_out, val_out, *whole = refs
    else:
        sum_in, val_in, sum_out, val_out, *whole = refs

    @pl.when(pl.program_id(0) == 0)
    def _():
        for j in range(n):
            lay_weights(place_ref, ws[2 * j], ws[2 * j + 1], whole[j])
        total = sum(dot(vs[j][...], whole[j][...]) for j in range(n))
        val_out[...] = total if first else total + val_in[...]

    total = sum(dot(xs[j][...], whole[j][...]) for j in range(n))
    sum_out[...] = total if first else total + sum_in[...]


WIDE = NY * NC * ROWS
TILE = 512


def project(where, train_x, val_x, zs, weights, sums, waits=()):
    n = len(zs)
    rows = train_x.shape[0]
    sum_specs = [pl.BlockSpec((TILE, HD), lambda i, p: (i, 0)), vmem((VSEQ, HD))]
    first = sums is None
    return call(
        functools.partial(project_kernel, n, first),
        (where,),
        (*[train_x] * n, *[val_x] * n, *weights, *([] if first else sums)),
        waits,
        (rows // TILE,),
        [pl.BlockSpec((TILE, WIDE), lambda i, p, dz=dz: (i, z_of(p, dz))) for dz in zs]
        + [pl.BlockSpec((VSEQ, WIDE), lambda i, p, dz=dz: (0, z_of(p, dz))) for dz in zs]
        + [vmem((NY, ROWS, HD))] * (2 * n)
        + ([] if first else sum_specs),
        sum_specs,
        [jax.ShapeDtypeStruct((rows, HD), f32), jax.ShapeDtypeStruct((VSEQ, HD), f32)],
        cost(2 * rows * n * WIDE * HD, 2 * rows * n * WIDE),
        [pltpu.VMEM((WIDE, HD), bf16)] * n,
    )


def grads_kernel(place_ref, x_ref, near_ref, far_ref, sum_ref, p_ref, target_ref, out_ref, whole):
    @pl.when(pl.program_id(0) == 0)
    def _():
        lay_weights(place_ref, near_ref, far_ref, whole)

    values = (sum_ref[...] + dot(x_ref[...], whole[...])).astype(bf16)
    attention = p_ref[0].reshape(GROUP * SEQ, SEQ)
    mixed = dot(attention, values)
    target = jnp.concatenate(
        [target_ref[:, h * HD : (h + 1) * HD] for h in range(GROUP)], axis=0
    ).astype(f32)
    residual = ((mixed - target) * (1.0 / SEQ)).astype(bf16)
    pulled = dot(residual, attention, ((0,), (0,)))
    out_ref[...] = pulled.astype(bf16)


def value_grads(where, train_x, weights, sums, attention, target, waits=()):
    rows = train_x.shape[0]
    return call(
        grads_kernel,
        (where,),
        (train_x, *weights, sums, attention, target),
        waits,
        (MEMBERS,),
        [
            pl.BlockSpec((SEQ, WIDE), lambda i, p: (i, z_of(p, 4))),
            vmem((NY, ROWS, HD)),
            vmem((NY, ROWS, HD)),
            pl.BlockSpec((SEQ, HD), lambda i, p: (i, 0)),
            pl.BlockSpec((1, GROUP, SEQ, SEQ), lambda i, p: (i, 0, 0, 0)),
            pl.BlockSpec((SEQ, GROUP * HD), lambda i, p: (i, 0)),
        ],
        pl.BlockSpec((HD, SEQ), lambda i, p: (0, i)),
        jax.ShapeDtypeStruct((HD, rows), bf16),
        cost(4 * rows * GROUP * SEQ * HD, 8 * 2**20),
        [pltpu.VMEM((WIDE, HD), bf16)],
    )


def val_kernel(place_ref, x_ref, near_ref, far_ref, sum_ref, p_ref, target_ref, out_ref, whole):
    lay_weights(place_ref, near_ref, far_ref, whole)
    values = (sum_ref[...] + dot(x_ref[...], whole[...])).astype(bf16)
    attention = p_ref[0].reshape(GROUP * VSEQ, VSEQ)
    target = jnp.concatenate(
        [target_ref[:, h * HD : (h + 1) * HD] for h in range(GROUP)], axis=0
    ).astype(f32)
    residual = (dot(attention, values) - target) * (1.0 / VSEQ)
    high = residual.astype(bf16)
    low = (residual - high.astype(f32)).astype(bf16)
    pulled = dot(high, attention, ((0,), (0,))) + dot(low, attention, ((0,), (0,)))
    out_ref[...] = pulled.astype(bf16)


def val_pulls(where, val_x, weights, sums, attention, target, waits=()):
    return call(
        val_kernel,
        (where,),
        (val_x, *weights, sums, attention, target),
        waits,
        (1,),
        [
            pl.BlockSpec((VSEQ, WIDE), lambda i, p: (0, z_of(p, 4))),
            vmem((NY, ROWS, HD)),
            vmem((NY, ROWS, HD)),
            vmem((VSEQ, HD)),
            vmem((1, GROUP, VSEQ, VSEQ)),
            vmem((VSEQ, GROUP * HD)),
        ],
        vmem((HD, VSEQ)),
        jax.ShapeDtypeStruct((HD, VSEQ), bf16),
        cost(10 * VSEQ * GROUP * VSEQ * HD, 2**20),
        [pltpu.VMEM((WIDE, HD), bf16)],
    )


def skills_kernel(place_ref, x_ref, grads_ref, theirs_ref, mine_ref, total):
    for dc, out_ref in ((1, theirs_ref), (0, mine_ref)):
        column = pl.multiple_of(lax.rem(place_ref[2] + dc, NC) * ROWS, ROWS)
        total[...] = jnp.zeros_like(total)
        for m in range(MEMBERS):
            tokens = slice(m * SEQ, (m + 1) * SEQ)
            product = dot(grads_ref[:, tokens], x_ref[tokens, pl.ds(column, ROWS)])
            total[place_ref[3 + m]] += product
        out_ref[0, 0] = total[...].reshape(SKILLS * HD, ROWS).astype(out_ref.dtype)


def skill_terms(where, train_x, grads, zs, waits=()):
    rows = train_x.shape[0]
    first, step = zs[0], zs[-1] - zs[0]
    out = pl.BlockSpec((1, 1, SKILLS * HD, ROWS), lambda i, j, p: (i, j, 0, 0))
    shape = (len(zs), NY, SKILLS * HD, ROWS)
    return call(
        skills_kernel,
        (where,),
        (train_x, grads),
        waits,
        (len(zs), NY),
        [
            pl.BlockSpec(
                (rows, NC * ROWS),
                lambda i, j, p: (0, z_of(p, first + i * step) * 2 + lax.rem(p[1] + j, NY)),
            ),
            pl.BlockSpec((HD, rows), lambda i, j, p: (0, 0)),
        ],
        [out, out],
        [jax.ShapeDtypeStruct(shape, bf16), jax.ShapeDtypeStruct(shape, f32)],
        cost(2 * rows * len(zs) * WIDE * HD, len(zs) * 5 * 2**20),
        [pltpu.VMEM((SKILLS, HD, ROWS), f32)],
    )


def stack_kernel(*refs):
    for i, ref in enumerate(refs[:-1]):
        refs[-1][i] = ref[...]


def stacked(blocks):
    shape = blocks[0].shape
    return call(
        stack_kernel,
        (),
        blocks,
        (),
        (1,),
        [vmem(shape)] * len(blocks),
        vmem((len(blocks),) + shape),
        jax.ShapeDtypeStruct((len(blocks),) + shape, blocks[0].dtype),
        cost(0, 2**20),
    )


def directions_kernel(place_ref, skill_ref, near_ref, far_ref, x_ref, out_ref):
    out_ref[...] = jnp.zeros_like(out_ref)
    for dz in range(NZ):
        for dy in range(NY):
            for dc, ref in enumerate((near_ref, far_ref)):
                f = z_of(place_ref, dz) * 4 + lax.rem(place_ref[1] + dy, NY) * 2 + lax.rem(place_ref[2] + dc, NC)
                tokens = x_ref[:, f].reshape(VSEQ, ROWS)
                out_ref[skill_ref[f]] += dot(ref[dz, dy], tokens)


def directions_of(where, val_skill, near, far, columns):
    return call(
        directions_kernel,
        (where, val_skill),
        (near, far, columns),
        (),
        (1,),
        [vmem(near.shape), vmem(far.shape), vmem(columns.shape)],
        vmem((SKILLS, HD, ROWS)),
        jax.ShapeDtypeStruct((SKILLS, HD, ROWS), f32),
        cost(2 * 4096 * ROWS * HD, 4 * 2**20),
    )


def local_kernel(mine_ref, theirs_ref, up_ref, down_ref, here_ref, there_ref, keep_ref, give_ref, local_ref):
    lane = lax.broadcasted_iota(jnp.int32, (1, HD), 1)
    local = jnp.zeros((1, HD), f32)
    for s in range(SKILLS):
        rows = slice(s * HD, (s + 1) * HD)
        totals = [
            mine_ref[0, dy, rows, :]
            + theirs_ref[0, dy, rows, :].astype(f32)
            + up_ref[dy, rows, :].astype(f32)
            + down_ref[dy, rows, :].astype(f32)
            for dy in range(NY)
        ]
        keep_ref[rows, :] = totals[0]
        give_ref[rows, :] = totals[1].astype(bf16)
        for v in range(SKILLS):
            product = totals[0] * here_ref[v] + totals[1] * there_ref[v].astype(f32)
            product = jnp.sum(product, axis=0, keepdims=True)
            entry = step_size * jnp.sum(product, axis=1, keepdims=True)
            local = jnp.where(lane == s * SKILLS + v, entry, local)
    local_ref[...] = local


def local_transfer(mine, theirs, up, down, here, there):
    operands = (mine, theirs, up, down, here, there)
    return call(
        local_kernel,
        (),
        operands,
        (),
        (1,),
        [vmem(o.shape) for o in operands],
        [vmem((SKILLS * HD, ROWS)), vmem((SKILLS * HD, ROWS)), vmem((1, HD))],
        [
            jax.ShapeDtypeStruct((SKILLS * HD, ROWS), f32),
            jax.ShapeDtypeStruct((SKILLS * HD, ROWS), bf16),
            jax.ShapeDtypeStruct((1, HD), f32),
        ],
        cost(2**22, 4 * 2**20),
    )


def finish_kernel(keep_ref, got_ref, grads_ref):
    for s in range(SKILLS):
        rows = slice(s * HD, (s + 1) * HD)
        grads_ref[s] = (keep_ref[rows, :] + got_ref[rows, :].astype(f32)).T.astype(bf16)


def finish(keep, got):
    return call(
        finish_kernel,
        (),
        (keep, got),
        (),
        (1,),
        [vmem(keep.shape), vmem(got.shape)],
        vmem((SKILLS, ROWS, HD)),
        jax.ShapeDtypeStruct((SKILLS, ROWS, HD), bf16),
        cost(2**20, 2**20),
    )


def sum_all(row):
    copies = jnp.broadcast_to(row, (NZ * NY * NC * NX * NL,) + row.shape)
    return jnp.sum(lax.all_to_all(copies, ("fsdp", "tp"), 0, 0), axis=0)


def on_device(
    train_x, train_q, train_k, train_target, train_skill, value_weight, val_x, val_q, val_k, val_target, val_skill
):
    f, t = lax.axis_index("fsdp"), lax.axis_index("tp")
    z, y, c = f // 4, (f // 2) % 2, f % 2
    own_skill = lax.dynamic_slice_in_dim(train_skill, f * MEMBERS, MEMBERS)
    where = jnp.concatenate([jnp.stack([z, y, c]).astype(jnp.int32), own_skill])

    part = VSEQ // 8
    own_tokens = lax.dynamic_slice_in_dim(val_x, t * part, part).reshape(part, 32, ROWS)
    crossed = lax.all_to_all(own_tokens.transpose(1, 0, 2), "fsdp", 0, 0)
    columns = lax.all_to_all(jnp.broadcast_to(crossed, (8,) + crossed.shape), "tp", 0, 0)

    def with_core(*blocks):
        return [w for block in blocks for w in (block, send(block, CORE))]

    val_attention = attend(val_q, val_k, VSEQ)
    attention = attend(train_q, train_k, SEQ, (val_attention,))
    pair = jnp.stack([value_weight, send(value_weight, YHI)])
    up1, down1 = send(pair, UP), send(pair, DOWN)
    up1, down1 = joined((up1, down1), (attention,))
    up2, down2 = send(up1, UP), send(down1, DOWN)
    sums = project(where, train_x, val_x, (0,), with_core(pair), None, (attention,))
    up2, down2 = joined((up2, down2), (sums[1],))
    up3, down3 = send(up2, UP), send(down2, DOWN)
    sums = project(where, train_x, val_x, (1, 7), with_core(down1, up1), sums)
    up3, down3 = joined((up3, down3), (sums[1], crossed))
    far_pair = jnp.stack([send(up3[0], UP), send(down3[1], DOWN)])
    sums = project(where, train_x, val_x, (2, 6), with_core(down2, up2), sums)
    sums = project(where, train_x, val_x, (3, 5), with_core(down3, up3), sums)
    last = with_core(far_pair)
    grads = value_grads(where, train_x, last, sums[0], attention, train_target)

    def terms(zs, *waits):
        theirs, mine = skill_terms(where, train_x, grads, zs, waits)
        return mine, send(theirs, CORE)

    def sum_of(parts, i, dy=slice(None)):
        return parts[0][i, dy] + parts[1][i, dy].astype(f32)

    parts = terms((4,))
    far0, far1 = sum_of(parts, 0, 0).astype(bf16), sum_of(parts, 0, 1).astype(bf16)
    up, down = send(far0, UP), send(far1, DOWN)
    parts = terms((3, 5), far0)
    pull = val_pulls(where, val_x, last, sums[1], val_attention, val_target, (up, down))
    pull = jnp.stack([pull, send(pull, YHI)])
    pulls = {0: pull}
    p_up, p_down = send(pull, UP), send(pull, DOWN)
    pulls[7], pulls[1] = p_up, p_down

    next_parts = terms((2, 6), up, down, pull)
    up = jnp.stack([sum_of(parts, 0, 0) + up.astype(f32), sum_of(parts, 0, 1)]).astype(bf16)
    down = jnp.stack([sum_of(parts, 1, 0), sum_of(parts, 1, 1) + down.astype(f32)]).astype(bf16)
    up, down = send(up, UP), send(down, DOWN)
    p_up, p_down = send(p_up, UP), send(p_down, DOWN)
    pulls[6], pulls[2] = p_up, p_down
    p_up, p_down = send(p_up, UP), send(p_down, DOWN)
    pulls[5], pulls[3] = p_up, p_down

    parts, next_parts = next_parts, terms((1, 7), up, down, p_up)
    up = send((sum_of(parts, 0) + up.astype(f32)).astype(bf16), UP)
    down = send((sum_of(parts, 1) + down.astype(f32)).astype(bf16), DOWN)
    pulls[4] = jnp.stack([send(p_up[0], UP), send(p_down[1], DOWN)])
    near_pulls = stacked([pulls[dz] for dz in range(NZ)])
    here = directions_of(where, val_skill, near_pulls, send(near_pulls, CORE), columns)

    parts, last_parts = next_parts, terms((0,), up, down, here)
    up = send((sum_of(parts, 0) + up.astype(f32)).astype(bf16), UP)
    down = send((sum_of(parts, 1) + down.astype(f32)).astype(bf16), DOWN)
    there = send(here.astype(bf16), YHI)
    keep, give, local = local_transfer(*last_parts, up, down, here, there)
    row = sum_all(local)
    skill_grads = finish(keep, send(give, YHI))
    return (skill_grads, row[0, : SKILLS * SKILLS].reshape(SKILLS, SKILLS))


def solution(mesh):
    placed = (
        P("fsdp", None),
        P("fsdp", "tp"),
        P("fsdp", "tp"),
        P("fsdp", "tp"),
        P(),
        P("fsdp", "tp"),
        P("fsdp", None),
        P("fsdp", "tp"),
        P("fsdp", "tp"),
        P("fsdp", "tp"),
        P(),
    )
    return jax.shard_map(
        on_device,
        mesh=mesh,
        in_specs=placed,
        out_specs=(P(None, "fsdp", "tp"), P()),
        check_vma=False,
    )
```

```python
import functools
import math

import jax
import jax.numpy as jnp
from jax import lax
from jax.experimental import pallas as pl
from jax.experimental.pallas import tpu as pltpu
from jax.sharding import PartitionSpec as P

HD = 128
GROUP = 8
SKILLS = 4
SEQ = 256
VSEQ = 128
MEMBERS = 4
NZ, NY, NC = 8, 2, 2
NX, NL = 4, 2
ROWS = 256

step_size = 0.01
bf16 = jnp.bfloat16
f32 = jnp.float32


def place(z, y, c):
    return (z % NZ) * 4 + (y % NY) * 2 + (c % NC)


def moves(fn):
    return [
        (place(z, y, c), place(*fn(z, y, c)))
        for z in range(NZ)
        for y in range(NY)
        for c in range(NC)
    ]


DIAGONAL = moves(lambda z, y, c: (z, y + 1, c + 1))
CORE = moves(lambda z, y, c: (z, y, c + 1))
YHI = moves(lambda z, y, c: (z, y + 1, c))
UP = moves(lambda z, y, c: (z + 1, y, c))
DOWN = moves(lambda z, y, c: (z - 1, y, c))


def send(value, way):
    return lax.ppermute(value, "fsdp", way)


def call(kernel, prefetched, operands, waits, grid, in_specs, out_specs, out_shape, cost_estimate, scratch=(), mib=50):
    first = len(prefetched) + len(operands)

    def body(*refs):
        kernel(*refs[:first], *refs[first + len(waits) :])

    return pl.pallas_call(
        body,
        grid_spec=pltpu.PrefetchScalarGridSpec(
            num_scalar_prefetch=len(prefetched),
            grid=grid,
            in_specs=list(in_specs) + [pl.BlockSpec(memory_space=pl.ANY)] * len(waits),
            out_specs=out_specs,
            scratch_shapes=list(scratch),
        ),
        out_shape=out_shape,
        compiler_params=pltpu.CompilerParams(vmem_limit_bytes=mib * 2**20),
        cost_estimate=cost_estimate,
    )(*prefetched, *operands, *waits)


def joined(values, waits):
    return pl.pallas_call(
        lambda *refs: None,
        in_specs=[pl.BlockSpec(memory_space=pl.ANY)] * (len(values) + len(waits)),
        out_specs=[pl.BlockSpec(memory_space=pl.ANY)] * len(values),
        out_shape=[jax.ShapeDtypeStruct(v.shape, v.dtype) for v in values],
        input_output_aliases={i: i for i in range(len(values))},
        compiler_params=pltpu.CompilerParams(vmem_limit_bytes=50 * 2**20),
        cost_estimate=cost(1, 1),
    )(*values, *waits)


def vmem(shape):
    return pl.BlockSpec(shape, lambda i, *_: (0,) * len(shape))


def cost(flops, moved, exps=0):
    return pl.CostEstimate(flops=flops // 64, bytes_accessed=moved // 64, transcendentals=exps // 64)


def dot(a, b, dims=((1,), (0,))):
    return lax.dot_general(a, b, (dims, ((), ())), preferred_element_type=f32)


def attend_kernel(length, q_ref, k_ref, p_ref):
    keys = k_ref[...]
    rows = lax.broadcasted_iota(jnp.int32, (length, length), 0)
    columns = lax.broadcasted_iota(jnp.int32, (length, length), 1)
    allowed = rows >= columns
    for h in range(GROUP):
        scores = dot(q_ref[:, h * HD : (h + 1) * HD], keys, ((1,), (1,)))
        scores = jnp.where(allowed, scores * (1.0 / math.sqrt(HD)), jnp.float32(-1e30))
        raised = jnp.exp(scores - jnp.max(scores, axis=-1, keepdims=True))
        total = jnp.sum(raised, axis=-1, keepdims=True)
        p_ref[0, h] = (raised * (1.0 / total)).astype(bf16)


def attend(queries, keys, length, waits=()):
    members = queries.shape[0] // length
    count = members * GROUP * length * length
    return call(
        functools.partial(attend_kernel, length),
        (),
        (queries, keys),
        waits,
        (members,),
        [
            pl.BlockSpec((length, GROUP * HD), lambda i: (i, 0)),
            pl.BlockSpec((length, HD), lambda i: (i, 0)),
        ],
        pl.BlockSpec((1, GROUP, length, length), lambda i: (i, 0, 0, 0)),
        jax.ShapeDtypeStruct((members, GROUP, length, length), bf16),
        cost(2 * count * HD, 4 * count, count),
    )


def z_of(place_ref, dz):
    return lax.rem(place_ref[0] + dz, NZ)


def lay_weights(place_ref, blocks, whole):
    for dc in range(NC):
        for dy in range(NY):
            y = lax.rem(place_ref[1] + dy, NY)
            c = lax.rem(place_ref[2] + dc, NC)
            row = pl.multiple_of((y * 2 + c) * ROWS, ROWS)
            whole[pl.ds(row, ROWS), :] = blocks[dc * NY + dy]


def project_kernel(n, first, place_ref, *refs):
    xs, refs = refs[:n], refs[n:]
    vs, refs = refs[:n], refs[n:]
    ws, refs = refs[:n], refs[n:]
    if first:
        sum_out, val_out, *whole = refs
    else:
        sum_in, val_in, sum_out, val_out, *whole = refs

    @pl.when(pl.program_id(0) == 0)
    def _():
        for j in range(n):
            lay_weights(place_ref, ws[j], whole[j])
        total = sum(dot(vs[j][...], whole[j][...]) for j in range(n))
        val_out[...] = total if first else total + val_in[...]

    total = sum(dot(xs[j][...], whole[j][...]) for j in range(n))
    sum_out[...] = total if first else total + sum_in[...]


WIDE = NY * NC * ROWS
TILE = 512


def project(where, train_x, val_x, zs, weights, sums, waits=()):
    n = len(zs)
    rows = train_x.shape[0]
    sum_specs = [pl.BlockSpec((TILE, HD), lambda i, p: (i, 0)), vmem((VSEQ, HD))]
    first = sums is None
    return call(
        functools.partial(project_kernel, n, first),
        (where,),
        (*[train_x] * n, *[val_x] * n, *weights, *([] if first else sums)),
        waits,
        (rows // TILE,),
        [pl.BlockSpec((TILE, WIDE), lambda i, p, dz=dz: (i, z_of(p, dz))) for dz in zs]
        + [pl.BlockSpec((VSEQ, WIDE), lambda i, p, dz=dz: (0, z_of(p, dz))) for dz in zs]
        + [vmem((NC * NY, ROWS, HD))] * n
        + ([] if first else sum_specs),
        sum_specs,
        [jax.ShapeDtypeStruct((rows, HD), f32), jax.ShapeDtypeStruct((VSEQ, HD), f32)],
        cost(2 * rows * n * WIDE * HD, 2 * rows * n * WIDE),
        [pltpu.VMEM((WIDE, HD), bf16)] * n,
    )


def grads_kernel(place_ref, x_ref, w_ref, sum_ref, p_ref, target_ref, out_ref, whole):
    @pl.when(pl.program_id(0) == 0)
    def _():
        lay_weights(place_ref, w_ref, whole)

    values = (sum_ref[...] + dot(x_ref[...], whole[...])).astype(bf16)
    attention = p_ref[0].reshape(GROUP * SEQ, SEQ)
    mixed = dot(attention, values)
    target = jnp.concatenate(
        [target_ref[:, h * HD : (h + 1) * HD] for h in range(GROUP)], axis=0
    ).astype(f32)
    residual = ((mixed - target) * (1.0 / SEQ)).astype(bf16)
    pulled = dot(residual, attention, ((0,), (0,)))
    out_ref[...] = pulled.astype(bf16)


def value_grads(where, train_x, weights, sums, attention, target, waits=()):
    rows = train_x.shape[0]
    return call(
        grads_kernel,
        (where,),
        (train_x, weights, sums, attention, target),
        waits,
        (MEMBERS,),
        [
            pl.BlockSpec((SEQ, WIDE), lambda i, p: (i, z_of(p, 4))),
            vmem((NC * NY, ROWS, HD)),
            pl.BlockSpec((SEQ, HD), lambda i, p: (i, 0)),
            pl.BlockSpec((1, GROUP, SEQ, SEQ), lambda i, p: (i, 0, 0, 0)),
            pl.BlockSpec((SEQ, GROUP * HD), lambda i, p: (i, 0)),
        ],
        pl.BlockSpec((HD, SEQ), lambda i, p: (0, i)),
        jax.ShapeDtypeStruct((HD, rows), bf16),
        cost(4 * rows * GROUP * SEQ * HD, 8 * 2**20),
        [pltpu.VMEM((WIDE, HD), bf16)],
    )


def val_kernel(place_ref, x_ref, w_ref, sum_ref, p_ref, target_ref, out_ref, whole):
    lay_weights(place_ref, w_ref, whole)
    values = (sum_ref[...] + dot(x_ref[...], whole[...])).astype(bf16)
    attention = p_ref[0].reshape(GROUP * VSEQ, VSEQ)
    target = jnp.concatenate(
        [target_ref[:, h * HD : (h + 1) * HD] for h in range(GROUP)], axis=0
    ).astype(f32)
    residual = (dot(attention, values) - target) * (1.0 / VSEQ)
    high = residual.astype(bf16)
    low = (residual - high.astype(f32)).astype(bf16)
    pulled = dot(high, attention, ((0,), (0,))) + dot(low, attention, ((0,), (0,)))
    out_ref[...] = pulled.astype(bf16)


def val_pulls(where, val_x, weights, sums, attention, target, waits=()):
    return call(
        val_kernel,
        (where,),
        (val_x, weights, sums, attention, target),
        waits,
        (1,),
        [
            pl.BlockSpec((VSEQ, WIDE), lambda i, p: (0, z_of(p, 4))),
            vmem((NC * NY, ROWS, HD)),
            vmem((VSEQ, HD)),
            vmem((1, GROUP, VSEQ, VSEQ)),
            vmem((VSEQ, GROUP * HD)),
        ],
        vmem((HD, VSEQ)),
        jax.ShapeDtypeStruct((HD, VSEQ), bf16),
        cost(10 * VSEQ * GROUP * VSEQ * HD, 2**20),
        [pltpu.VMEM((WIDE, HD), bf16)],
    )


def pick_kernel(place_ref, x_ref, out_ref, sems):
    copies = []
    for i in range(NZ * NY):
        column = pl.multiple_of((2 * i + 1 - place_ref[2]) * ROWS, ROWS)
        source = x_ref.at[:, pl.ds(column, ROWS)]
        copies.append(pltpu.make_async_copy(source, out_ref.at[:, i * ROWS : (i + 1) * ROWS], sems.at[i]))
    for copy in copies:
        copy.start()
    for copy in copies:
        copy.wait()


def other_core_columns(where, train_x, waits=()):
    rows, columns = train_x.shape
    anywhere = pl.BlockSpec(memory_space=pl.ANY)
    return call(
        pick_kernel,
        (where,),
        (train_x,),
        waits,
        (1,),
        [anywhere],
        anywhere,
        jax.ShapeDtypeStruct((rows, columns // NC), bf16),
        cost(0, 2 * rows * columns),
        [pltpu.SemaphoreType.DMA((NZ * NY,))],
    )


def skills_kernel(place_ref, own_x, other_x, own_grads, other_grads, out_ref, total):
    total[...] = jnp.zeros_like(total)
    for k, (x_ref, grads_ref) in enumerate(((own_x, own_grads), (other_x, other_grads))):
        for m in range(MEMBERS):
            tokens = slice(m * SEQ, (m + 1) * SEQ)
            total[place_ref[3 + k * MEMBERS + m]] += dot(grads_ref[:, tokens], x_ref[tokens, :])
    out_ref[0, 0] = total[...].reshape(SKILLS * HD, ROWS)


def skill_terms(where, own_x, other_x, grads, zs, waits=()):
    rows = own_x.shape[0]
    first, step = zs[0], zs[-1] - zs[0]

    def pair_of(i, j, p):
        return z_of(p, first + i * step) * 2 + lax.rem(p[1] + j, NY)

    return call(
        skills_kernel,
        (where,),
        (own_x, other_x, *grads),
        waits,
        (len(zs), NY),
        [
            pl.BlockSpec((rows, ROWS), lambda i, j, p: (0, pair_of(i, j, p) * 2 + p[2])),
            pl.BlockSpec((rows, ROWS), lambda i, j, p: (0, pair_of(i, j, p))),
            pl.BlockSpec((HD, rows), lambda i, j, p: (0, 0)),
            pl.BlockSpec((HD, rows), lambda i, j, p: (0, 0)),
        ],
        pl.BlockSpec((1, 1, SKILLS * HD, ROWS), lambda i, j, p: (i, j, 0, 0)),
        jax.ShapeDtypeStruct((len(zs), NY, SKILLS * HD, ROWS), f32),
        cost(2 * rows * len(zs) * WIDE * HD, len(zs) * 5 * 2**20),
        [pltpu.VMEM((SKILLS, HD, ROWS), f32)],
    )


HALF = SKILLS * HD


def step_kernel(step, mine_ref, up_ref, down_ref, up_out, down_out):
    if step == 1:
        up_out[:HALF, :] = mine_ref[0, 0].astype(bf16)
        down_out[:HALF, :] = mine_ref[0, 1].astype(bf16)
        up_out[HALF:, :] = up_ref[...]
        down_out[HALF:, :] = down_ref[...]
        return
    for dy in range(NY):
        rows = slice(dy * HALF, (dy + 1) * HALF)
        if step == 2:
            came = (up_ref if dy == 0 else None, down_ref if dy == 1 else None)
            there = slice(0, HALF)
        else:
            came, there = (up_ref, down_ref), rows
        for k, (ref, out) in enumerate(zip(came, (up_out, down_out))):
            total = mine_ref[k, dy]
            if ref is not None:
                total = total + ref[there, :].astype(f32)
            out[rows, :] = total.astype(bf16)
    if step < 4:
        for ref, out in ((up_ref, up_out), (down_ref, down_out)):
            out[NY * HALF :, :] = ref[ref.shape[0] - HD :, :]


def ring_step(step, mine, up, down):
    rows = {1: HALF + HD, 2: NY * HALF + HD, 3: NY * HALF + HD, 4: NY * HALF}[step]
    shape = (rows, ROWS)
    operands = (mine, up, down)
    up, down = call(
        functools.partial(step_kernel, step),
        (),
        operands,
        (),
        (1,),
        [vmem(o.shape) for o in operands],
        [vmem(shape), vmem(shape)],
        [jax.ShapeDtypeStruct(shape, bf16)] * 2,
        cost(2**20, 4 * 2**20),
    )
    return up, (send(up, UP), send(down, DOWN))


def stack_kernel(*refs):
    for i, ref in enumerate(refs[:-1]):
        refs[-1][i] = ref[...]


def stacked(arrays):
    tails = [pl.BlockSpec((HD, ROWS), lambda i, n=a.shape[0] // HD - 1: (n, 0)) for a in arrays]
    return call(
        stack_kernel,
        (),
        arrays,
        (),
        (1,),
        tails,
        vmem((len(arrays), HD, ROWS)),
        jax.ShapeDtypeStruct((len(arrays), HD, ROWS), bf16),
        cost(0, 2**20),
    )


def directions_kernel(place_ref, skill_ref, near_ref, far_ref, x_ref, out_ref):
    out_ref[...] = jnp.zeros_like(out_ref)
    for dz in range(NZ):
        for dy in range(NY):
            for dc, ref in enumerate((near_ref, far_ref)):
                f = z_of(place_ref, dz) * 4 + lax.rem(place_ref[1] + dy, NY) * 2 + lax.rem(place_ref[2] + dc, NC)
                tokens = x_ref[:, f].reshape(VSEQ, ROWS)
                out_ref[skill_ref[f]] += dot(ref[dz, :, dy * HD : (dy + 1) * HD], tokens)


def directions_of(where, val_skill, near, far, columns):
    return call(
        directions_kernel,
        (where, val_skill),
        (near, far, columns),
        (),
        (1,),
        [vmem(near.shape), vmem(far.shape), vmem(columns.shape)],
        vmem((SKILLS, HD, ROWS)),
        jax.ShapeDtypeStruct((SKILLS, HD, ROWS), f32),
        cost(2 * 4096 * ROWS * HD, 4 * 2**20),
    )


def local_kernel(mine_ref, up_ref, down_ref, here_ref, there_ref, keep_ref, give_ref, local_ref):
    lane = lax.broadcasted_iota(jnp.int32, (1, HD), 1)
    local = jnp.zeros((1, HD), f32)
    for s in range(SKILLS):
        rows = slice(s * HD, (s + 1) * HD)
        totals = [
            mine_ref[0, dy, rows, :]
            + up_ref[dy * HALF + s * HD : dy * HALF + (s + 1) * HD, :].astype(f32)
            + down_ref[dy * HALF + s * HD : dy * HALF + (s + 1) * HD, :].astype(f32)
            for dy in range(NY)
        ]
        keep_ref[rows, :] = totals[0]
        give_ref[rows, :] = totals[1].astype(bf16)
        for v in range(SKILLS):
            product = totals[0] * here_ref[v] + totals[1] * there_ref[v].astype(f32)
            product = jnp.sum(product, axis=0, keepdims=True)
            entry = step_size * jnp.sum(product, axis=1, keepdims=True)
            local = jnp.where(lane == s * SKILLS + v, entry, local)
    local_ref[...] = local


def local_transfer(mine, up, down, here, there):
    operands = (mine, up, down, here, there)
    return call(
        local_kernel,
        (),
        operands,
        (),
        (1,),
        [vmem(o.shape) for o in operands],
        [vmem((SKILLS * HD, ROWS)), vmem((SKILLS * HD, ROWS)), vmem((1, HD))],
        [
            jax.ShapeDtypeStruct((SKILLS * HD, ROWS), f32),
            jax.ShapeDtypeStruct((SKILLS * HD, ROWS), bf16),
            jax.ShapeDtypeStruct((1, HD), f32),
        ],
        cost(2**22, 4 * 2**20),
    )


def finish_kernel(keep_ref, got_ref, grads_ref):
    for s in range(SKILLS):
        rows = slice(s * HD, (s + 1) * HD)
        grads_ref[s] = (keep_ref[rows, :] + got_ref[rows, :].astype(f32)).T.astype(bf16)


def finish(keep, got):
    return call(
        finish_kernel,
        (),
        (keep, got),
        (),
        (1,),
        [vmem(keep.shape), vmem(got.shape)],
        vmem((SKILLS, ROWS, HD)),
        jax.ShapeDtypeStruct((SKILLS, ROWS, HD), bf16),
        cost(2**20, 2**20),
    )


def sum_all(row):
    copies = jnp.broadcast_to(row, (NZ * NY * NC * NX * NL,) + row.shape)
    return jnp.sum(lax.all_to_all(copies, ("fsdp", "tp"), 0, 0), axis=0)


def on_device(
    train_x, train_q, train_k, train_target, train_skill, value_weight, val_x, val_q, val_k, val_target, val_skill
):
    f, t = lax.axis_index("fsdp"), lax.axis_index("tp")
    z, y, c = f // 4, (f // 2) % 2, f % 2
    own_skill = lax.dynamic_slice_in_dim(train_skill, f * MEMBERS, MEMBERS)
    other_skill = lax.dynamic_slice_in_dim(train_skill, (f + 1 - 2 * c) * MEMBERS, MEMBERS)
    where = jnp.concatenate([jnp.stack([z, y, c]).astype(jnp.int32), own_skill, other_skill])

    part = VSEQ // 8
    own_tokens = lax.dynamic_slice_in_dim(val_x, t * part, part).reshape(part, 32, ROWS)
    crossed = lax.all_to_all(own_tokens.transpose(1, 0, 2), "fsdp", 0, 0)
    columns = lax.all_to_all(jnp.broadcast_to(crossed, (8,) + crossed.shape), "tp", 0, 0)

    own = value_weight
    quad = jnp.stack([own, send(own, YHI), send(own, CORE), send(own, DIAGONAL)])
    val_attention = attend(val_q, val_k, VSEQ)
    attention = attend(train_q, train_k, SEQ, (val_attention, quad))
    up1, down1 = send(quad, UP), send(quad, DOWN)
    up1, down1 = joined((up1, down1), (attention,))
    up2, down2 = send(up1, UP), send(down1, DOWN)
    sums = project(where, train_x, val_x, (0,), [quad], None, (attention, up1))
    picked = other_core_columns(where, train_x, (up1,))
    other_x = send(picked, CORE)
    up2, down2 = joined((up2, down2), (sums[1], picked))
    up3, down3 = send(up2, UP), send(down2, DOWN)
    sums = project(where, train_x, val_x, (1, 7), [down1, up1], sums)
    up3, down3 = joined((up3, down3), (sums[1], crossed))
    last = jnp.concatenate([send(up3[:2], UP), send(down3[2:], DOWN)])
    sums = project(where, train_x, val_x, (2, 6), [down2, up2], sums)
    sums = project(where, train_x, val_x, (3, 5), [down3, up3], sums)
    own_pull = val_pulls(where, val_x, last, sums[1], val_attention, val_target)
    pull = jnp.concatenate([own_pull, send(own_pull, YHI)], axis=1)
    p_up, p_down = send(pull, UP), send(pull, DOWN)
    grads = value_grads(where, train_x, last, sums[0], attention, train_target, (own_pull,))
    grads = (grads, send(grads, CORE))

    def terms(zs, *waits):
        return skill_terms(where, train_x, other_x, grads, zs, waits)

    pulls = {0: pull, 1: p_down, 7: p_up}
    sent, (up, down) = ring_step(1, terms((4,)), p_up, p_down)
    mine = terms((3, 5), sent)
    pulls[6], pulls[2] = up, down
    sent, (up, down) = ring_step(2, mine, up, down)
    mine = terms((2, 6), sent)
    pulls[5], pulls[3] = up, down
    sent, (up, down) = ring_step(3, mine, up, down)
    mine = terms((1, 7), sent)
    pulls[4] = up
    sent, (up, down) = ring_step(4, mine, up, down)
    near_pulls = stacked([pulls[dz] for dz in range(NZ)])
    here = directions_of(where, val_skill, near_pulls, send(near_pulls, CORE), columns)
    there = send(here.astype(bf16), YHI)
    keep, give, local = local_transfer(terms((0,), sent, here), up, down, here, there)
    row = sum_all(local)
    skill_grads = finish(keep, send(give, YHI))
    return (skill_grads, row[0, : SKILLS * SKILLS].reshape(SKILLS, SKILLS))


def solution(mesh):
    placed = (
        P("fsdp", None),
        P("fsdp", "tp"),
        P("fsdp", "tp"),
        P("fsdp", "tp"),
        P(),
        P("fsdp", "tp"),
        P("fsdp", None),
        P("fsdp", "tp"),
        P("fsdp", "tp"),
        P("fsdp", "tp"),
        P(),
    )
    return jax.shard_map(
        on_device,
        mesh=mesh,
        in_specs=placed,
        out_specs=(P(None, "fsdp", "tp"), P()),
        check_vma=False,
    )
```

```python
import functools
import math

import jax
import jax.numpy as jnp
from jax import lax
from jax.experimental import pallas as pl
from jax.experimental.pallas import tpu as pltpu
from jax.sharding import PartitionSpec as P

HD = 128
GROUP = 8
SKILLS = 4
SEQ = 256
VSEQ = 128
MEMBERS = 4
NZ, NY, NC = 8, 2, 2
NX, NL = 4, 2
ROWS = 256

step_size = 0.01
bf16 = jnp.bfloat16
f32 = jnp.float32


def place(z, y, c):
    return (z % NZ) * 4 + (y % NY) * 2 + (c % NC)


def moves(fn):
    return [
        (place(z, y, c), place(*fn(z, y, c)))
        for z in range(NZ)
        for y in range(NY)
        for c in range(NC)
    ]


DIAGONAL = moves(lambda z, y, c: (z, y + 1, c + 1))
CORE = moves(lambda z, y, c: (z, y, c + 1))
YHI = moves(lambda z, y, c: (z, y + 1, c))
UP = moves(lambda z, y, c: (z + 1, y, c))
DOWN = moves(lambda z, y, c: (z - 1, y, c))


def send(value, way):
    return lax.ppermute(value, "fsdp", way)


def call(kernel, prefetched, operands, waits, grid, in_specs, out_specs, out_shape, cost_estimate, scratch=(), mib=50):
    first = len(prefetched) + len(operands)

    def body(*refs):
        kernel(*refs[:first], *refs[first + len(waits) :])

    return pl.pallas_call(
        body,
        grid_spec=pltpu.PrefetchScalarGridSpec(
            num_scalar_prefetch=len(prefetched),
            grid=grid,
            in_specs=list(in_specs) + [pl.BlockSpec(memory_space=pl.ANY)] * len(waits),
            out_specs=out_specs,
            scratch_shapes=list(scratch),
        ),
        out_shape=out_shape,
        compiler_params=pltpu.CompilerParams(vmem_limit_bytes=mib * 2**20),
        cost_estimate=cost_estimate,
    )(*prefetched, *operands, *waits)


def joined(values, waits):
    return pl.pallas_call(
        lambda *refs: None,
        in_specs=[pl.BlockSpec(memory_space=pl.ANY)] * (len(values) + len(waits)),
        out_specs=[pl.BlockSpec(memory_space=pl.ANY)] * len(values),
        out_shape=[jax.ShapeDtypeStruct(v.shape, v.dtype) for v in values],
        input_output_aliases={i: i for i in range(len(values))},
        compiler_params=pltpu.CompilerParams(vmem_limit_bytes=50 * 2**20),
        cost_estimate=cost(1, 1),
    )(*values, *waits)


def vmem(shape):
    return pl.BlockSpec(shape, lambda i, *_: (0,) * len(shape))


def cost(flops, moved, exps=0):
    return pl.CostEstimate(flops=flops // 64, bytes_accessed=moved // 64, transcendentals=exps // 64)


def dot(a, b, dims=((1,), (0,))):
    return lax.dot_general(a, b, (dims, ((), ())), preferred_element_type=f32)


def attend_kernel(length, q_ref, k_ref, p_ref):
    keys = k_ref[...]
    rows = lax.broadcasted_iota(jnp.int32, (length, length), 0)
    columns = lax.broadcasted_iota(jnp.int32, (length, length), 1)
    allowed = rows >= columns
    for h in range(GROUP):
        scores = dot(q_ref[:, h * HD : (h + 1) * HD], keys, ((1,), (1,)))
        scores = jnp.where(allowed, scores * (1.0 / math.sqrt(HD)), jnp.float32(-1e30))
        raised = jnp.exp(scores - jnp.max(scores, axis=-1, keepdims=True))
        total = jnp.sum(raised, axis=-1, keepdims=True)
        p_ref[0, h] = (raised * (1.0 / total)).astype(bf16)


def attend(queries, keys, length, waits=()):
    members = queries.shape[0] // length
    count = members * GROUP * length * length
    return call(
        functools.partial(attend_kernel, length),
        (),
        (queries, keys),
        waits,
        (members,),
        [
            pl.BlockSpec((length, GROUP * HD), lambda i: (i, 0)),
            pl.BlockSpec((length, HD), lambda i: (i, 0)),
        ],
        pl.BlockSpec((1, GROUP, length, length), lambda i: (i, 0, 0, 0)),
        jax.ShapeDtypeStruct((members, GROUP, length, length), bf16),
        cost(2 * count * HD, 4 * count, count),
    )


def z_of(place_ref, dz):
    return lax.rem(place_ref[0] + dz, NZ)


def lay_weights(place_ref, blocks, whole):
    for dc in range(NC):
        for dy in range(NY):
            y = lax.rem(place_ref[1] + dy, NY)
            c = lax.rem(place_ref[2] + dc, NC)
            row = pl.multiple_of((y * 2 + c) * ROWS, ROWS)
            whole[pl.ds(row, ROWS), :] = blocks[dc * NY + dy]


def project_kernel(n, extra, first, place_ref, *refs):
    xs, refs = refs[: n + extra], refs[n + extra :]
    vs, refs = refs[:n], refs[n:]
    ws, refs = refs[:n], refs[n:]
    if first:
        sum_out, val_out, pick_out, *whole = refs
    else:
        sum_in, val_in, sum_out, val_out, pick_out, *whole = refs

    @pl.when(pl.program_id(0) == 0)
    def _():
        for j in range(n):
            lay_weights(place_ref, ws[j], whole[j])
        total = sum(dot(vs[j][...], whole[j][...]) for j in range(n))
        val_out[...] = total if first else total + val_in[...]

    total = sum(dot(xs[j][...], whole[j][...]) for j in range(n))
    sum_out[...] = total if first else total + sum_in[...]
    for j, x_ref in enumerate(xs[n if extra else 0 :]):
        for y in range(NY):
            column = pl.multiple_of((y * 2 + 1 - place_ref[2]) * ROWS, ROWS)
            pick_out[j, :, y * ROWS : (y + 1) * ROWS] = x_ref[:, pl.ds(column, ROWS)]


WIDE = NY * NC * ROWS
TILE = 512


def project(where, train_x, val_x, zs, weights, sums, waits=(), others=()):
    n, extra = len(zs), len(others)
    rows = train_x.shape[0]
    sum_specs = [pl.BlockSpec((TILE, HD), lambda i, p: (i, 0)), vmem((VSEQ, HD))]
    first = sums is None
    picks = extra or n
    pick_spec = pl.BlockSpec((picks, TILE, NY * ROWS), lambda i, p: (0, i, 0))
    return call(
        functools.partial(project_kernel, n, extra, first),
        (where,),
        (*[train_x] * (n + extra), *[val_x] * n, *weights, *([] if first else sums)),
        waits,
        (rows // TILE,),
        [pl.BlockSpec((TILE, WIDE), lambda i, p, dz=dz: (i, z_of(p, dz))) for dz in (*zs, *others)]
        + [pl.BlockSpec((VSEQ, WIDE), lambda i, p, dz=dz: (0, z_of(p, dz))) for dz in zs]
        + [vmem((NC * NY, ROWS, HD))] * n
        + ([] if first else sum_specs),
        sum_specs + [pick_spec],
        [
            jax.ShapeDtypeStruct((rows, HD), f32),
            jax.ShapeDtypeStruct((VSEQ, HD), f32),
            jax.ShapeDtypeStruct((picks, rows, NY * ROWS), bf16),
        ],
        cost(2 * rows * n * WIDE * HD, 2 * rows * n * WIDE),
        [pltpu.VMEM((WIDE, HD), bf16)] * n,
    )


def grads_kernel(place_ref, x_ref, w_ref, sum_ref, p_ref, target_ref, out_ref, whole):
    @pl.when(pl.program_id(0) == 0)
    def _():
        lay_weights(place_ref, w_ref, whole)

    values = (sum_ref[...] + dot(x_ref[...], whole[...])).astype(bf16)
    attention = p_ref[0].reshape(GROUP * SEQ, SEQ)
    mixed = dot(attention, values)
    target = jnp.concatenate(
        [target_ref[:, h * HD : (h + 1) * HD] for h in range(GROUP)], axis=0
    ).astype(f32)
    residual = ((mixed - target) * (1.0 / SEQ)).astype(bf16)
    pulled = dot(residual, attention, ((0,), (0,)))
    out_ref[...] = pulled.astype(bf16)


def value_grads(where, train_x, weights, sums, attention, target, waits=()):
    rows = train_x.shape[0]
    return call(
        grads_kernel,
        (where,),
        (train_x, weights, sums, attention, target),
        waits,
        (MEMBERS,),
        [
            pl.BlockSpec((SEQ, WIDE), lambda i, p: (i, z_of(p, 4))),
            vmem((NC * NY, ROWS, HD)),
            pl.BlockSpec((SEQ, HD), lambda i, p: (i, 0)),
            pl.BlockSpec((1, GROUP, SEQ, SEQ), lambda i, p: (i, 0, 0, 0)),
            pl.BlockSpec((SEQ, GROUP * HD), lambda i, p: (i, 0)),
        ],
        pl.BlockSpec((HD, SEQ), lambda i, p: (0, i)),
        jax.ShapeDtypeStruct((HD, rows), bf16),
        cost(4 * rows * GROUP * SEQ * HD, 8 * 2**20),
        [pltpu.VMEM((WIDE, HD), bf16)],
    )


def val_kernel(place_ref, x_ref, w_ref, sum_ref, p_ref, target_ref, out_ref, whole):
    lay_weights(place_ref, w_ref, whole)
    values = (sum_ref[...] + dot(x_ref[...], whole[...])).astype(bf16)
    attention = p_ref[0].reshape(GROUP * VSEQ, VSEQ)
    target = jnp.concatenate(
        [target_ref[:, h * HD : (h + 1) * HD] for h in range(GROUP)], axis=0
    ).astype(f32)
    residual = (dot(attention, values) - target) * (1.0 / VSEQ)
    high = residual.astype(bf16)
    low = (residual - high.astype(f32)).astype(bf16)
    pulled = dot(high, attention, ((0,), (0,))) + dot(low, attention, ((0,), (0,)))
    out_ref[...] = pulled.astype(bf16)


def val_pulls(where, val_x, weights, sums, attention, target, waits=()):
    return call(
        val_kernel,
        (where,),
        (val_x, weights, sums, attention, target),
        waits,
        (1,),
        [
            pl.BlockSpec((VSEQ, WIDE), lambda i, p: (0, z_of(p, 4))),
            vmem((NC * NY, ROWS, HD)),
            vmem((VSEQ, HD)),
            vmem((1, GROUP, VSEQ, VSEQ)),
            vmem((VSEQ, GROUP * HD)),
        ],
        vmem((HD, VSEQ)),
        jax.ShapeDtypeStruct((HD, VSEQ), bf16),
        cost(10 * VSEQ * GROUP * VSEQ * HD, 2**20),
        [pltpu.VMEM((WIDE, HD), bf16)],
    )


def skills_kernel(place_ref, own_x, other_x, own_grads, other_grads, out_ref, total):
    total[...] = jnp.zeros_like(total)
    for k, (x_ref, grads_ref) in enumerate(((own_x, own_grads), (other_x.at[0], other_grads))):
        for m in range(MEMBERS):
            tokens = slice(m * SEQ, (m + 1) * SEQ)
            total[place_ref[3 + k * MEMBERS + m]] += dot(grads_ref[:, tokens], x_ref[tokens, :])
    out_ref[0, 0] = total[...].reshape(SKILLS * HD, ROWS)


def skill_terms(where, own_x, other_x, grads, zs, waits=()):
    rows = own_x.shape[0]
    first, step = zs[0], zs[-1] - zs[0]

    def pair_of(i, j, p):
        return z_of(p, first + i * step) * 2 + lax.rem(p[1] + j, NY)

    return call(
        skills_kernel,
        (where,),
        (own_x, other_x, *grads),
        waits,
        (len(zs), NY),
        [
            pl.BlockSpec((rows, ROWS), lambda i, j, p: (0, pair_of(i, j, p) * 2 + p[2])),
            pl.BlockSpec((1, rows, ROWS), lambda i, j, p: (i, 0, lax.rem(p[1] + j, NY))),
            pl.BlockSpec((HD, rows), lambda i, j, p: (0, 0)),
            pl.BlockSpec((HD, rows), lambda i, j, p: (0, 0)),
        ],
        pl.BlockSpec((1, 1, SKILLS * HD, ROWS), lambda i, j, p: (i, j, 0, 0)),
        jax.ShapeDtypeStruct((len(zs), NY, SKILLS * HD, ROWS), f32),
        cost(2 * rows * len(zs) * WIDE * HD, len(zs) * 5 * 2**20),
        [pltpu.VMEM((SKILLS, HD, ROWS), f32)],
    )


HALF = SKILLS * HD


def step_kernel(step, mine_ref, up_ref, down_ref, up_out, down_out):
    if step == 1:
        up_out[:HALF, :] = mine_ref[0, 0].astype(bf16)
        down_out[:HALF, :] = mine_ref[0, 1].astype(bf16)
        up_out[HALF:, :] = up_ref[...]
        down_out[HALF:, :] = down_ref[...]
        return
    for dy in range(NY):
        rows = slice(dy * HALF, (dy + 1) * HALF)
        if step == 2:
            came = (up_ref if dy == 0 else None, down_ref if dy == 1 else None)
            there = slice(0, HALF)
        else:
            came, there = (up_ref, down_ref), rows
        for k, (ref, out) in enumerate(zip(came, (up_out, down_out))):
            total = mine_ref[k, dy]
            if ref is not None:
                total = total + ref[there, :].astype(f32)
            out[rows, :] = total.astype(bf16)
    if step < 4:
        for ref, out in ((up_ref, up_out), (down_ref, down_out)):
            out[NY * HALF :, :] = ref[ref.shape[0] - HD :, :]


def ring_step(step, mine, up, down):
    rows = {1: HALF + HD, 2: NY * HALF + HD, 3: NY * HALF + HD, 4: NY * HALF}[step]
    shape = (rows, ROWS)
    operands = (mine, up, down)
    up, down = call(
        functools.partial(step_kernel, step),
        (),
        operands,
        (),
        (1,),
        [vmem(o.shape) for o in operands],
        [vmem(shape), vmem(shape)],
        [jax.ShapeDtypeStruct(shape, bf16)] * 2,
        cost(2**20, 4 * 2**20),
    )
    return up, (send(up, UP), send(down, DOWN))


def stack_kernel(*refs):
    for i, ref in enumerate(refs[:-1]):
        refs[-1][i] = ref[...]


def stacked(arrays, waits=()):
    tails = [pl.BlockSpec((HD, ROWS), lambda i, n=a.shape[0] // HD - 1: (n, 0)) for a in arrays]
    return call(
        stack_kernel,
        (),
        arrays,
        waits,
        (1,),
        tails,
        vmem((len(arrays), HD, ROWS)),
        jax.ShapeDtypeStruct((len(arrays), HD, ROWS), bf16),
        cost(0, 2**20),
    )


def copies_kernel(from_ref, to_ref):
    to_ref[0] = from_ref[...]


def copies(array, count, waits):
    return call(
        copies_kernel,
        (),
        (array,),
        waits,
        (count,),
        [vmem(array.shape)],
        pl.BlockSpec((1,) + array.shape, lambda i: (i, 0, 0, 0)),
        jax.ShapeDtypeStruct((count,) + array.shape, array.dtype),
        cost(0, 2**20),
    )


def directions_kernel(place_ref, skill_ref, near_ref, far_ref, x_ref, out_ref):
    out_ref[...] = jnp.zeros_like(out_ref)
    for dz in range(NZ):
        for dy in range(NY):
            for dc, ref in enumerate((near_ref, far_ref)):
                f = z_of(place_ref, dz) * 4 + lax.rem(place_ref[1] + dy, NY) * 2 + lax.rem(place_ref[2] + dc, NC)
                tokens = x_ref[:, f].reshape(VSEQ, ROWS)
                out_ref[skill_ref[f]] += dot(ref[dz, :, dy * HD : (dy + 1) * HD], tokens)


def directions_of(where, val_skill, near, far, columns):
    return call(
        directions_kernel,
        (where, val_skill),
        (near, far, columns),
        (),
        (1,),
        [vmem(near.shape), vmem(far.shape), vmem(columns.shape)],
        vmem((SKILLS, HD, ROWS)),
        jax.ShapeDtypeStruct((SKILLS, HD, ROWS), f32),
        cost(2 * 4096 * ROWS * HD, 4 * 2**20),
    )


def local_kernel(mine_ref, up_ref, down_ref, here_ref, there_ref, keep_ref, give_ref, local_ref):
    lane = lax.broadcasted_iota(jnp.int32, (1, HD), 1)
    local = jnp.zeros((1, HD), f32)
    for s in range(SKILLS):
        rows = slice(s * HD, (s + 1) * HD)
        totals = [
            mine_ref[0, dy, rows, :]
            + up_ref[dy * HALF + s * HD : dy * HALF + (s + 1) * HD, :].astype(f32)
            + down_ref[dy * HALF + s * HD : dy * HALF + (s + 1) * HD, :].astype(f32)
            for dy in range(NY)
        ]
        keep_ref[rows, :] = totals[0]
        give_ref[rows, :] = totals[1].astype(bf16)
        for v in range(SKILLS):
            product = totals[0] * here_ref[v] + totals[1] * there_ref[v].astype(f32)
            product = jnp.sum(product, axis=0, keepdims=True)
            entry = step_size * jnp.sum(product, axis=1, keepdims=True)
            local = jnp.where(lane == s * SKILLS + v, entry, local)
    local_ref[...] = local


def local_transfer(mine, up, down, here, there):
    operands = (mine, up, down, here, there)
    return call(
        local_kernel,
        (),
        operands,
        (),
        (1,),
        [vmem(o.shape) for o in operands],
        [vmem((SKILLS * HD, ROWS)), vmem((SKILLS * HD, ROWS)), vmem((1, HD))],
        [
            jax.ShapeDtypeStruct((SKILLS * HD, ROWS), f32),
            jax.ShapeDtypeStruct((SKILLS * HD, ROWS), bf16),
            jax.ShapeDtypeStruct((1, HD), f32),
        ],
        cost(2**22, 4 * 2**20),
    )


def finish_kernel(keep_ref, got_ref, grads_ref):
    for s in range(SKILLS):
        rows = slice(s * HD, (s + 1) * HD)
        grads_ref[s] = (keep_ref[rows, :] + got_ref[rows, :].astype(f32)).T.astype(bf16)


def finish(keep, got):
    return call(
        finish_kernel,
        (),
        (keep, got),
        (),
        (1,),
        [vmem(keep.shape), vmem(got.shape)],
        vmem((SKILLS, ROWS, HD)),
        jax.ShapeDtypeStruct((SKILLS, ROWS, HD), bf16),
        cost(2**20, 2**20),
    )


def sum_all(row):
    copies = jnp.broadcast_to(row, (NZ * NY * NC * NX * NL,) + row.shape)
    return jnp.sum(lax.all_to_all(copies, ("fsdp", "tp"), 0, 0), axis=0)


def on_device(
    train_x, train_q, train_k, train_target, train_skill, value_weight, val_x, val_q, val_k, val_target, val_skill
):
    f, t = lax.axis_index("fsdp"), lax.axis_index("tp")
    z, y, c = f // 4, (f // 2) % 2, f % 2
    own_skill = lax.dynamic_slice_in_dim(train_skill, f * MEMBERS, MEMBERS)
    other_skill = lax.dynamic_slice_in_dim(train_skill, (f + 1 - 2 * c) * MEMBERS, MEMBERS)
    where = jnp.concatenate([jnp.stack([z, y, c]).astype(jnp.int32), own_skill, other_skill])

    part = VSEQ // 8
    own_tokens = lax.dynamic_slice_in_dim(val_x, t * part, part).reshape(part, 32, ROWS)
    crossed = lax.all_to_all(own_tokens.transpose(1, 0, 2), "fsdp", 0, 0)

    own = value_weight
    quad = jnp.stack([own, send(own, YHI), send(own, CORE), send(own, DIAGONAL)])
    val_attention = attend(val_q, val_k, VSEQ)
    attention = attend(train_q, train_k, SEQ, (val_attention, quad))
    up1, down1 = send(quad, UP), send(quad, DOWN)
    up1, down1 = joined((up1, down1), (attention,))
    up2, down2 = send(up1, UP), send(down1, DOWN)
    *sums, picked = project(where, train_x, val_x, (0,), [quad], None, (attention, up1), (4, 0))
    other_x = {(4,): send(picked[:1], CORE), (0,): send(picked[1:], CORE)}
    up2, down2 = joined((up2, down2), (sums[1],))
    up3, down3 = send(up2, UP), send(down2, DOWN)
    *sums, picked = project(where, train_x, val_x, (1, 7), [down1, up1], sums)
    other_x[1, 7] = send(picked, CORE)
    up3, down3 = joined((up3, down3), (sums[1], crossed))
    last = jnp.concatenate([send(up3[:2], UP), send(down3[2:], DOWN)])
    *sums, picked = project(where, train_x, val_x, (2, 6), [down2, up2], sums)
    other_x[2, 6] = send(picked, CORE)
    *sums, picked = project(where, train_x, val_x, (3, 5), [down3, up3], sums)
    other_x[3, 5] = send(picked, CORE)
    own_pull = val_pulls(where, val_x, last, sums[1], val_attention, val_target)
    pull = jnp.concatenate([own_pull, send(own_pull, YHI)], axis=1)
    p_up, p_down = send(pull, UP), send(pull, DOWN)
    grads = value_grads(where, train_x, last, sums[0], attention, train_target, (own_pull,))
    grads = (grads, send(grads, CORE))

    def terms(zs, *waits):
        return skill_terms(where, train_x, other_x[zs], grads, zs, waits)

    pulls = {0: pull, 1: p_down, 7: p_up}
    sent, (up, down) = ring_step(1, terms((4,)), p_up, p_down)
    mine = terms((3, 5), sent)
    columns = lax.all_to_all(copies(crossed, NX * NL, (sent,)), "tp", 0, 0)
    pulls[6], pulls[2] = up, down
    sent, (up, down) = ring_step(2, mine, up, down)
    mine = terms((2, 6), sent)
    pulls[5], pulls[3] = up, down
    sent, (up, down) = ring_step(3, mine, up, down)
    mine = terms((1, 7), sent)
    pulls[4] = up
    sent, (up, down) = ring_step(4, mine, up, down)
    near_pulls = stacked([pulls[dz] for dz in range(NZ)], (sent,))
    here = directions_of(where, val_skill, near_pulls, send(near_pulls, CORE), columns)
    there = send(here.astype(bf16), YHI)
    keep, give, local = local_transfer(terms((0,), sent, here), up, down, here, there)
    row = sum_all(local)
    skill_grads = finish(keep, send(give, YHI))
    return (skill_grads, row[0, : SKILLS * SKILLS].reshape(SKILLS, SKILLS))


def solution(mesh):
    placed = (
        P("fsdp", None),
        P("fsdp", "tp"),
        P("fsdp", "tp"),
        P("fsdp", "tp"),
        P(),
        P("fsdp", "tp"),
        P("fsdp", None),
        P("fsdp", "tp"),
        P("fsdp", "tp"),
        P("fsdp", "tp"),
        P(),
    )
    return jax.shard_map(
        on_device,
        mesh=mesh,
        in_specs=placed,
        out_specs=(P(None, "fsdp", "tp"), P()),
        check_vma=False,
    )
```

```python
import functools
import math

import jax
import jax.numpy as jnp
from jax import lax
from jax.experimental import pallas as pl
from jax.experimental.pallas import tpu as pltpu
from jax.sharding import PartitionSpec as P

HD = 128
GROUP = 8
SKILLS = 4
SEQ = 256
VSEQ = 128
MEMBERS = 4
NZ, NY, NC = 8, 2, 2
NX, NL = 4, 2
ROWS = 256

step_size = 0.01
bf16 = jnp.bfloat16
f32 = jnp.float32


def place(z, y, c):
    return (z % NZ) * 4 + (y % NY) * 2 + (c % NC)


def moves(fn):
    return [
        (place(z, y, c), place(*fn(z, y, c)))
        for z in range(NZ)
        for y in range(NY)
        for c in range(NC)
    ]


DIAGONAL = moves(lambda z, y, c: (z, y + 1, c + 1))
CORE = moves(lambda z, y, c: (z, y, c + 1))
YHI = moves(lambda z, y, c: (z, y + 1, c))
UP = moves(lambda z, y, c: (z + 1, y, c))
DOWN = moves(lambda z, y, c: (z - 1, y, c))


def send(value, way):
    return lax.ppermute(value, "fsdp", way)


def call(kernel, prefetched, operands, waits, grid, in_specs, out_specs, out_shape, cost_estimate, scratch=(), mib=50):
    first = len(prefetched) + len(operands)

    def body(*refs):
        kernel(*refs[:first], *refs[first + len(waits) :])

    return pl.pallas_call(
        body,
        grid_spec=pltpu.PrefetchScalarGridSpec(
            num_scalar_prefetch=len(prefetched),
            grid=grid,
            in_specs=list(in_specs) + [pl.BlockSpec(memory_space=pl.ANY)] * len(waits),
            out_specs=out_specs,
            scratch_shapes=list(scratch),
        ),
        out_shape=out_shape,
        compiler_params=pltpu.CompilerParams(vmem_limit_bytes=mib * 2**20),
        cost_estimate=cost_estimate,
    )(*prefetched, *operands, *waits)


def joined(values, waits):
    return pl.pallas_call(
        lambda *refs: None,
        in_specs=[pl.BlockSpec(memory_space=pl.ANY)] * (len(values) + len(waits)),
        out_specs=[pl.BlockSpec(memory_space=pl.ANY)] * len(values),
        out_shape=[jax.ShapeDtypeStruct(v.shape, v.dtype) for v in values],
        input_output_aliases={i: i for i in range(len(values))},
        compiler_params=pltpu.CompilerParams(vmem_limit_bytes=50 * 2**20),
        cost_estimate=cost(1, 1),
    )(*values, *waits)


def vmem(shape):
    return pl.BlockSpec(shape, lambda i, *_: (0,) * len(shape))


def cost(flops, moved, exps=0):
    return pl.CostEstimate(flops=flops // 4096, bytes_accessed=moved // 4096, transcendentals=exps // 4096)


def dot(a, b, dims=((1,), (0,))):
    return lax.dot_general(a, b, (dims, ((), ())), preferred_element_type=f32)


def attend_kernel(length, q_ref, k_ref, p_ref):
    keys = k_ref[...]
    rows = lax.broadcasted_iota(jnp.int32, (length, length), 0)
    columns = lax.broadcasted_iota(jnp.int32, (length, length), 1)
    allowed = rows >= columns
    for h in range(GROUP):
        scores = dot(q_ref[:, h * HD : (h + 1) * HD], keys, ((1,), (1,)))
        scores = jnp.where(allowed, scores * (1.0 / math.sqrt(HD)), jnp.float32(-1e30))
        raised = jnp.exp(scores - jnp.max(scores, axis=-1, keepdims=True))
        total = jnp.sum(raised, axis=-1, keepdims=True)
        p_ref[0, h] = (raised * (1.0 / total)).astype(bf16)


def attend(queries, keys, length, waits=()):
    members = queries.shape[0] // length
    count = members * GROUP * length * length
    return call(
        functools.partial(attend_kernel, length),
        (),
        (queries, keys),
        waits,
        (members,),
        [
            pl.BlockSpec((length, GROUP * HD), lambda i: (i, 0)),
            pl.BlockSpec((length, HD), lambda i: (i, 0)),
        ],
        pl.BlockSpec((1, GROUP, length, length), lambda i: (i, 0, 0, 0)),
        jax.ShapeDtypeStruct((members, GROUP, length, length), bf16),
        cost(2 * count * HD, 4 * count, count),
    )


def z_of(place_ref, dz):
    return lax.rem(place_ref[0] + dz, NZ)


def lay_weights(place_ref, blocks, whole):
    for dc in range(NC):
        for dy in range(NY):
            y = lax.rem(place_ref[1] + dy, NY)
            c = lax.rem(place_ref[2] + dc, NC)
            row = pl.multiple_of((y * 2 + c) * ROWS, ROWS)
            whole[pl.ds(row, ROWS), :] = blocks[dc * NY + dy]


def project_kernel(n, extra, first, place_ref, *refs):
    xs, refs = refs[: n + extra], refs[n + extra :]
    vs, refs = refs[:n], refs[n:]
    ws, refs = refs[:n], refs[n:]
    if first:
        sum_out, val_out, pick_out, *whole = refs
    else:
        sum_in, val_in, sum_out, val_out, pick_out, *whole = refs

    @pl.when(pl.program_id(0) == 0)
    def _():
        for j in range(n):
            lay_weights(place_ref, ws[j], whole[j])
        total = sum(dot(vs[j][...], whole[j][...]) for j in range(n))
        val_out[...] = total if first else total + val_in[...]

    total = sum(dot(xs[j][...], whole[j][...]) for j in range(n))
    sum_out[...] = total if first else total + sum_in[...]
    for j, x_ref in enumerate(xs[n if extra else 0 :]):
        for y in range(NY):
            column = pl.multiple_of((y * 2 + 1 - place_ref[2]) * ROWS, ROWS)
            pick_out[j, :, y * ROWS : (y + 1) * ROWS] = x_ref[:, pl.ds(column, ROWS)]


WIDE = NY * NC * ROWS
TILE = 512


def project(where, train_x, val_x, zs, weights, sums, waits=(), others=()):
    n, extra = len(zs), len(others)
    rows = train_x.shape[0]
    sum_specs = [pl.BlockSpec((TILE, HD), lambda i, p: (i, 0)), vmem((VSEQ, HD))]
    first = sums is None
    picks = extra or n
    pick_spec = pl.BlockSpec((picks, TILE, NY * ROWS), lambda i, p: (0, i, 0))
    return call(
        functools.partial(project_kernel, n, extra, first),
        (where,),
        (*[train_x] * (n + extra), *[val_x] * n, *weights, *([] if first else sums)),
        waits,
        (rows // TILE,),
        [pl.BlockSpec((TILE, WIDE), lambda i, p, dz=dz: (i, z_of(p, dz))) for dz in (*zs, *others)]
        + [pl.BlockSpec((VSEQ, WIDE), lambda i, p, dz=dz: (0, z_of(p, dz))) for dz in zs]
        + [vmem((NC * NY, ROWS, HD))] * n
        + ([] if first else sum_specs),
        sum_specs + [pick_spec],
        [
            jax.ShapeDtypeStruct((rows, HD), f32),
            jax.ShapeDtypeStruct((VSEQ, HD), f32),
            jax.ShapeDtypeStruct((picks, rows, NY * ROWS), bf16),
        ],
        cost(2 * rows * n * WIDE * HD, 2 * rows * n * WIDE),
        [pltpu.VMEM((WIDE, HD), bf16)] * n,
    )


def grads_kernel(place_ref, x_ref, w_ref, sum_ref, p_ref, target_ref, out_ref, whole):
    @pl.when(pl.program_id(0) == 0)
    def _():
        lay_weights(place_ref, w_ref, whole)

    values = (sum_ref[...] + dot(x_ref[...], whole[...])).astype(bf16)
    attention = p_ref[0].reshape(GROUP * SEQ, SEQ)
    mixed = dot(attention, values)
    target = jnp.concatenate(
        [target_ref[:, h * HD : (h + 1) * HD] for h in range(GROUP)], axis=0
    ).astype(f32)
    residual = ((mixed - target) * (1.0 / SEQ)).astype(bf16)
    pulled = dot(residual, attention, ((0,), (0,)))
    out_ref[...] = pulled.astype(bf16)


def value_grads(where, train_x, weights, sums, attention, target, waits=()):
    rows = train_x.shape[0]
    return call(
        grads_kernel,
        (where,),
        (train_x, weights, sums, attention, target),
        waits,
        (MEMBERS,),
        [
            pl.BlockSpec((SEQ, WIDE), lambda i, p: (i, z_of(p, 4))),
            vmem((NC * NY, ROWS, HD)),
            pl.BlockSpec((SEQ, HD), lambda i, p: (i, 0)),
            pl.BlockSpec((1, GROUP, SEQ, SEQ), lambda i, p: (i, 0, 0, 0)),
            pl.BlockSpec((SEQ, GROUP * HD), lambda i, p: (i, 0)),
        ],
        pl.BlockSpec((HD, SEQ), lambda i, p: (0, i)),
        jax.ShapeDtypeStruct((HD, rows), bf16),
        cost(4 * rows * GROUP * SEQ * HD, 8 * 2**20),
        [pltpu.VMEM((WIDE, HD), bf16)],
    )


def val_kernel(place_ref, x_ref, w_ref, sum_ref, p_ref, target_ref, out_ref, whole):
    lay_weights(place_ref, w_ref, whole)
    values = (sum_ref[...] + dot(x_ref[...], whole[...])).astype(bf16)
    attention = p_ref[0].reshape(GROUP * VSEQ, VSEQ)
    target = jnp.concatenate(
        [target_ref[:, h * HD : (h + 1) * HD] for h in range(GROUP)], axis=0
    ).astype(f32)
    residual = (dot(attention, values) - target) * (1.0 / VSEQ)
    high = residual.astype(bf16)
    low = (residual - high.astype(f32)).astype(bf16)
    pulled = dot(high, attention, ((0,), (0,))) + dot(low, attention, ((0,), (0,)))
    out_ref[...] = pulled.astype(bf16)


def val_pulls(where, val_x, weights, sums, attention, target, waits=()):
    return call(
        val_kernel,
        (where,),
        (val_x, weights, sums, attention, target),
        waits,
        (1,),
        [
            pl.BlockSpec((VSEQ, WIDE), lambda i, p: (0, z_of(p, 4))),
            vmem((NC * NY, ROWS, HD)),
            vmem((VSEQ, HD)),
            vmem((1, GROUP, VSEQ, VSEQ)),
            vmem((VSEQ, GROUP * HD)),
        ],
        vmem((HD, VSEQ)),
        jax.ShapeDtypeStruct((HD, VSEQ), bf16),
        cost(10 * VSEQ * GROUP * VSEQ * HD, 2**20),
        [pltpu.VMEM((WIDE, HD), bf16)],
    )


def skills_kernel(place_ref, own_x, other_x, own_grads, other_grads, out_ref, total):
    total[...] = jnp.zeros_like(total)
    for k, (x_ref, grads_ref) in enumerate(((own_x, own_grads), (other_x.at[0], other_grads))):
        for m in range(MEMBERS):
            tokens = slice(m * SEQ, (m + 1) * SEQ)
            total[place_ref[3 + k * MEMBERS + m]] += dot(grads_ref[:, tokens], x_ref[tokens, :])
    out_ref[0, 0] = total[...].reshape(SKILLS * HD, ROWS)


def skill_terms(where, own_x, other_x, grads, zs, waits=()):
    rows = own_x.shape[0]
    first, step = zs[0], zs[-1] - zs[0]

    def pair_of(i, j, p):
        return z_of(p, first + i * step) * 2 + lax.rem(p[1] + j, NY)

    return call(
        skills_kernel,
        (where,),
        (own_x, other_x, *grads),
        waits,
        (len(zs), NY),
        [
            pl.BlockSpec((rows, ROWS), lambda i, j, p: (0, pair_of(i, j, p) * 2 + p[2])),
            pl.BlockSpec((1, rows, ROWS), lambda i, j, p: (i, 0, lax.rem(p[1] + j, NY))),
            pl.BlockSpec((HD, rows), lambda i, j, p: (0, 0)),
            pl.BlockSpec((HD, rows), lambda i, j, p: (0, 0)),
        ],
        pl.BlockSpec((1, 1, SKILLS * HD, ROWS), lambda i, j, p: (i, j, 0, 0)),
        jax.ShapeDtypeStruct((len(zs), NY, SKILLS * HD, ROWS), f32),
        cost(2 * rows * len(zs) * WIDE * HD, len(zs) * 5 * 2**20),
        [pltpu.VMEM((SKILLS, HD, ROWS), f32)],
    )


HALF = SKILLS * HD


def step_kernel(step, mine_ref, up_ref, down_ref, up_out, down_out):
    if step == 1:
        up_out[:HALF, :] = mine_ref[0, 0].astype(bf16)
        down_out[:HALF, :] = mine_ref[0, 1].astype(bf16)
        up_out[HALF:, :] = up_ref[...]
        down_out[HALF:, :] = down_ref[...]
        return
    for dy in range(NY):
        rows = slice(dy * HALF, (dy + 1) * HALF)
        if step == 2:
            came = (up_ref if dy == 0 else None, down_ref if dy == 1 else None)
            there = slice(0, HALF)
        else:
            came, there = (up_ref, down_ref), rows
        for k, (ref, out) in enumerate(zip(came, (up_out, down_out))):
            total = mine_ref[k, dy]
            if ref is not None:
                total = total + ref[there, :].astype(f32)
            out[rows, :] = total.astype(bf16)
    if step < 4:
        for ref, out in ((up_ref, up_out), (down_ref, down_out)):
            out[NY * HALF :, :] = ref[ref.shape[0] - HD :, :]


def ring_step(step, mine, up, down):
    rows = {1: HALF + HD, 2: NY * HALF + HD, 3: NY * HALF + HD, 4: NY * HALF}[step]
    shape = (rows, ROWS)
    operands = (mine, up, down)
    up, down = call(
        functools.partial(step_kernel, step),
        (),
        operands,
        (),
        (1,),
        [vmem(o.shape) for o in operands],
        [vmem(shape), vmem(shape)],
        [jax.ShapeDtypeStruct(shape, bf16)] * 2,
        cost(2**20, 4 * 2**20),
    )
    return up, (send(up, UP), send(down, DOWN))


def stack_kernel(*refs):
    for i, ref in enumerate(refs[:-1]):
        refs[-1][i] = ref[...]


def stacked(arrays, waits=()):
    tails = [pl.BlockSpec((HD, ROWS), lambda i, n=a.shape[0] // HD - 1: (n, 0)) for a in arrays]
    return call(
        stack_kernel,
        (),
        arrays,
        waits,
        (1,),
        tails,
        vmem((len(arrays), HD, ROWS)),
        jax.ShapeDtypeStruct((len(arrays), HD, ROWS), bf16),
        cost(0, 2**20),
    )


def copies_kernel(from_ref, to_ref):
    to_ref[0] = from_ref[...]


def copies(array, count, waits):
    return call(
        copies_kernel,
        (),
        (array,),
        waits,
        (count,),
        [vmem(array.shape)],
        pl.BlockSpec((1,) + array.shape, lambda i: (i, 0, 0, 0)),
        jax.ShapeDtypeStruct((count,) + array.shape, array.dtype),
        cost(0, 2**20),
    )


def directions_kernel(place_ref, skill_ref, near_ref, far_ref, x_ref, out_ref):
    out_ref[...] = jnp.zeros_like(out_ref)
    for dz in range(NZ):
        for dy in range(NY):
            for dc, ref in enumerate((near_ref, far_ref)):
                f = z_of(place_ref, dz) * 4 + lax.rem(place_ref[1] + dy, NY) * 2 + lax.rem(place_ref[2] + dc, NC)
                tokens = x_ref[:, f].reshape(VSEQ, ROWS)
                out_ref[skill_ref[f]] += dot(ref[dz, :, dy * HD : (dy + 1) * HD], tokens)


def directions_of(where, val_skill, near, far, columns):
    return call(
        directions_kernel,
        (where, val_skill),
        (near, far, columns),
        (),
        (1,),
        [vmem(near.shape), vmem(far.shape), vmem(columns.shape)],
        vmem((SKILLS, HD, ROWS)),
        jax.ShapeDtypeStruct((SKILLS, HD, ROWS), f32),
        cost(2 * 4096 * ROWS * HD, 4 * 2**20),
    )


def local_kernel(mine_ref, up_ref, down_ref, here_ref, there_ref, keep_ref, give_ref, local_ref):
    lane = lax.broadcasted_iota(jnp.int32, (1, HD), 1)
    local = jnp.zeros((1, HD), f32)
    for s in range(SKILLS):
        rows = slice(s * HD, (s + 1) * HD)
        totals = [
            mine_ref[0, dy, rows, :]
            + up_ref[dy * HALF + s * HD : dy * HALF + (s + 1) * HD, :].astype(f32)
            + down_ref[dy * HALF + s * HD : dy * HALF + (s + 1) * HD, :].astype(f32)
            for dy in range(NY)
        ]
        keep_ref[rows, :] = totals[0]
        give_ref[rows, :] = totals[1].astype(bf16)
        for v in range(SKILLS):
            product = totals[0] * here_ref[v] + totals[1] * there_ref[v].astype(f32)
            product = jnp.sum(product, axis=0, keepdims=True)
            entry = step_size * jnp.sum(product, axis=1, keepdims=True)
            local = jnp.where(lane == s * SKILLS + v, entry, local)
    local_ref[...] = local


def local_transfer(mine, up, down, here, there):
    operands = (mine, up, down, here, there)
    return call(
        local_kernel,
        (),
        operands,
        (),
        (1,),
        [vmem(o.shape) for o in operands],
        [vmem((SKILLS * HD, ROWS)), vmem((SKILLS * HD, ROWS)), vmem((1, HD))],
        [
            jax.ShapeDtypeStruct((SKILLS * HD, ROWS), f32),
            jax.ShapeDtypeStruct((SKILLS * HD, ROWS), bf16),
            jax.ShapeDtypeStruct((1, HD), f32),
        ],
        cost(2**22, 4 * 2**20),
    )


def finish_kernel(keep_ref, got_ref, grads_ref):
    for s in range(SKILLS):
        rows = slice(s * HD, (s + 1) * HD)
        grads_ref[s] = (keep_ref[rows, :] + got_ref[rows, :].astype(f32)).T.astype(bf16)


def finish(keep, got):
    return call(
        finish_kernel,
        (),
        (keep, got),
        (),
        (1,),
        [vmem(keep.shape), vmem(got.shape)],
        vmem((SKILLS, ROWS, HD)),
        jax.ShapeDtypeStruct((SKILLS, ROWS, HD), bf16),
        cost(2**20, 2**20),
    )


def rows_kernel(rows_ref, out_ref):
    out_ref[...] = jnp.sum(rows_ref[...], axis=0)


def sum_rows(rows, waits):
    return call(
        rows_kernel,
        (),
        (rows,),
        waits,
        (1,),
        [vmem(rows.shape)],
        vmem(rows.shape[1:]),
        jax.ShapeDtypeStruct(rows.shape[1:], f32),
        cost(2**20, 2**20),
    )


def on_device(
    train_x, train_q, train_k, train_target, train_skill, value_weight, val_x, val_q, val_k, val_target, val_skill
):
    f, t = lax.axis_index("fsdp"), lax.axis_index("tp")
    z, y, c = f // 4, (f // 2) % 2, f % 2
    own_skill = lax.dynamic_slice_in_dim(train_skill, f * MEMBERS, MEMBERS)
    other_skill = lax.dynamic_slice_in_dim(train_skill, (f + 1 - 2 * c) * MEMBERS, MEMBERS)
    where = jnp.concatenate([jnp.stack([z, y, c]).astype(jnp.int32), own_skill, other_skill])

    part = VSEQ // 8
    own_tokens = lax.dynamic_slice_in_dim(val_x, t * part, part).reshape(part, 32, ROWS)
    crossed = lax.all_to_all(own_tokens.transpose(1, 0, 2), "fsdp", 0, 0)

    own = value_weight
    quad = jnp.stack([own, send(own, YHI), send(own, CORE), send(own, DIAGONAL)])
    val_attention = attend(val_q, val_k, VSEQ)
    attention = attend(train_q, train_k, SEQ, (val_attention, quad))
    up1, down1 = send(quad, UP), send(quad, DOWN)
    up1, down1 = joined((up1, down1), (attention,))
    up2, down2 = send(up1, UP), send(down1, DOWN)
    *sums, picked = project(where, train_x, val_x, (0,), [quad], None, (attention, up1, crossed), (4, 0))
    other_x = {(4,): send(picked[:1], CORE), (0,): send(picked[1:], CORE)}
    up2, down2 = joined((up2, down2), (sums[1],))
    up3, down3 = send(up2, UP), send(down2, DOWN)
    *sums, picked = project(where, train_x, val_x, (1, 7), [down1, up1], sums)
    other_x[1, 7] = send(picked, CORE)
    up3, down3 = joined((up3, down3), (sums[1],))
    last = jnp.concatenate([send(up3[:2], UP), send(down3[2:], DOWN)])
    *sums, picked = project(where, train_x, val_x, (2, 6), [down2, up2], sums)
    other_x[2, 6] = send(picked, CORE)
    *sums, picked = project(where, train_x, val_x, (3, 5), [down3, up3], sums)
    other_x[3, 5] = send(picked, CORE)
    own_pull = val_pulls(where, val_x, last, sums[1], val_attention, val_target)
    pull = jnp.concatenate([own_pull, send(own_pull, YHI)], axis=1)
    p_up, p_down = send(pull, UP), send(pull, DOWN)
    grads = value_grads(where, train_x, last, sums[0], attention, train_target, (own_pull,))
    grads = (grads, send(grads, CORE))

    def terms(zs, *waits):
        return skill_terms(where, train_x, other_x[zs], grads, zs, waits)

    pulls = {0: pull, 1: p_down, 7: p_up}
    sent, (up, down) = ring_step(1, terms((4,)), p_up, p_down)
    mine = terms((3, 5), sent)
    columns = lax.all_to_all(copies(crossed, NX * NL, (sent,)), "tp", 0, 0)
    pulls[6], pulls[2] = up, down
    sent, (up, down) = ring_step(2, mine, up, down)
    mine = terms((2, 6), sent)
    pulls[5], pulls[3] = up, down
    sent, (up, down) = ring_step(3, mine, up, down)
    mine = terms((1, 7), sent)
    pulls[4] = up
    sent, (up, down) = ring_step(4, mine, up, down)
    near_pulls = stacked([pulls[dz] for dz in range(NZ)], (sent,))
    here = directions_of(where, val_skill, near_pulls, send(near_pulls, CORE), columns)
    there = send(here.astype(bf16), YHI)
    keep, give, local = local_transfer(terms((0,), sent, here), up, down, here, there)
    rows = jnp.broadcast_to(local, (NZ * NY * NC * NX * NL,) + local.shape)
    rows = lax.all_to_all(rows, ("fsdp", "tp"), 0, 0)
    skill_grads = finish(keep, send(give, YHI))
    row = sum_rows(rows, (skill_grads,))
    return (skill_grads, row[0, : SKILLS * SKILLS].reshape(SKILLS, SKILLS))


def solution(mesh):
    placed = (
        P("fsdp", None),
        P("fsdp", "tp"),
        P("fsdp", "tp"),
        P("fsdp", "tp"),
        P(),
        P("fsdp", "tp"),
        P("fsdp", None),
        P("fsdp", "tp"),
        P("fsdp", "tp"),
        P("fsdp", "tp"),
        P(),
    )
    return jax.shard_map(
        on_device,
        mesh=mesh,
        in_specs=placed,
        out_specs=(P(None, "fsdp", "tp"), P()),
        check_vma=False,
    )
```

```python
import functools
import math

import jax
import jax.numpy as jnp
from jax import lax
from jax.experimental import pallas as pl
from jax.experimental.pallas import tpu as pltpu
from jax.sharding import PartitionSpec as P

HD = 128
GROUP = 8
SKILLS = 4
SEQ = 256
VSEQ = 128
MEMBERS = 4
NZ, NY, NC = 8, 2, 2
NX, NL = 4, 2
ROWS = 256

step_size = 0.01
bf16 = jnp.bfloat16
f32 = jnp.float32


def place(z, y, c):
    return (z % NZ) * 4 + (y % NY) * 2 + (c % NC)


def moves(fn):
    return [
        (place(z, y, c), place(*fn(z, y, c)))
        for z in range(NZ)
        for y in range(NY)
        for c in range(NC)
    ]


DIAGONAL = moves(lambda z, y, c: (z, y + 1, c + 1))
CORE = moves(lambda z, y, c: (z, y, c + 1))
YHI = moves(lambda z, y, c: (z, y + 1, c))
UP = moves(lambda z, y, c: (z + 1, y, c))
DOWN = moves(lambda z, y, c: (z - 1, y, c))


def send(value, way):
    return lax.ppermute(value, "fsdp", way)


def call(kernel, prefetched, operands, waits, grid, in_specs, out_specs, out_shape, cost_estimate, scratch=(), mib=50):
    first = len(prefetched) + len(operands)

    def body(*refs):
        kernel(*refs[:first], *refs[first + len(waits) :])

    return pl.pallas_call(
        body,
        grid_spec=pltpu.PrefetchScalarGridSpec(
            num_scalar_prefetch=len(prefetched),
            grid=grid,
            in_specs=list(in_specs) + [pl.BlockSpec(memory_space=pl.ANY)] * len(waits),
            out_specs=out_specs,
            scratch_shapes=list(scratch),
        ),
        out_shape=out_shape,
        compiler_params=pltpu.CompilerParams(vmem_limit_bytes=mib * 2**20),
        cost_estimate=cost_estimate,
    )(*prefetched, *operands, *waits)


def joined(values, waits):
    return pl.pallas_call(
        lambda *refs: None,
        in_specs=[pl.BlockSpec(memory_space=pl.ANY)] * (len(values) + len(waits)),
        out_specs=[pl.BlockSpec(memory_space=pl.ANY)] * len(values),
        out_shape=[jax.ShapeDtypeStruct(v.shape, v.dtype) for v in values],
        input_output_aliases={i: i for i in range(len(values))},
        compiler_params=pltpu.CompilerParams(vmem_limit_bytes=50 * 2**20),
        cost_estimate=cost(1, 1),
    )(*values, *waits)


def vmem(shape):
    return pl.BlockSpec(shape, lambda i, *_: (0,) * len(shape))


def cost(flops, moved, exps=0):
    return pl.CostEstimate(flops=flops // 4096, bytes_accessed=moved // 4096, transcendentals=exps // 4096)


def dot(a, b, dims=((1,), (0,))):
    return lax.dot_general(a, b, (dims, ((), ())), preferred_element_type=f32)


def attend_kernel(length, q_ref, k_ref, p_ref):
    keys = k_ref[...]
    rows = lax.broadcasted_iota(jnp.int32, (length, length), 0)
    columns = lax.broadcasted_iota(jnp.int32, (length, length), 1)
    allowed = rows >= columns
    for h in range(GROUP):
        scores = dot(q_ref[:, h * HD : (h + 1) * HD], keys, ((1,), (1,)))
        scores = jnp.where(allowed, scores * (1.0 / math.sqrt(HD)), jnp.float32(-1e30))
        raised = jnp.exp(scores - jnp.max(scores, axis=-1, keepdims=True))
        total = jnp.sum(raised, axis=-1, keepdims=True)
        p_ref[0, h] = (raised * (1.0 / total)).astype(bf16)


def attend(queries, keys, length, waits=()):
    members = queries.shape[0] // length
    count = members * GROUP * length * length
    return call(
        functools.partial(attend_kernel, length),
        (),
        (queries, keys),
        waits,
        (members,),
        [
            pl.BlockSpec((length, GROUP * HD), lambda i: (i, 0)),
            pl.BlockSpec((length, HD), lambda i: (i, 0)),
        ],
        pl.BlockSpec((1, GROUP, length, length), lambda i: (i, 0, 0, 0)),
        jax.ShapeDtypeStruct((members, GROUP, length, length), bf16),
        cost(2 * count * HD, 4 * count, count),
    )


def z_of(place_ref, dz):
    return lax.rem(place_ref[0] + dz, NZ)


def lay_weights(place_ref, blocks, whole):
    for dc in range(NC):
        for dy in range(NY):
            y = lax.rem(place_ref[1] + dy, NY)
            c = lax.rem(place_ref[2] + dc, NC)
            row = pl.multiple_of((y * 2 + c) * ROWS, ROWS)
            whole[pl.ds(row, ROWS), :] = blocks[dc * NY + dy]


def project_kernel(n, extra, first, place_ref, *refs):
    xs, refs = refs[: n + extra], refs[n + extra :]
    vs, refs = refs[:n], refs[n:]
    ws, refs = refs[:n], refs[n:]
    if first:
        sum_out, val_out, pick_out, *whole = refs
    else:
        sum_in, val_in, sum_out, val_out, pick_out, *whole = refs

    @pl.when(pl.program_id(0) == 0)
    def _():
        for j in range(n):
            lay_weights(place_ref, ws[j], whole[j])
        total = sum(dot(vs[j][...], whole[j][...]) for j in range(n))
        val_out[...] = total if first else total + val_in[...]

    total = sum(dot(xs[j][...], whole[j][...]) for j in range(n))
    sum_out[...] = total if first else total + sum_in[...]
    for j, x_ref in enumerate(xs[n if extra else 0 :]):
        for y in range(NY):
            column = pl.multiple_of((y * 2 + 1 - place_ref[2]) * ROWS, ROWS)
            pick_out[j, :, y * ROWS : (y + 1) * ROWS] = x_ref[:, pl.ds(column, ROWS)]


WIDE = NY * NC * ROWS
TILE = 512


def project(where, train_x, val_x, zs, weights, sums, waits=(), others=()):
    n, extra = len(zs), len(others)
    rows = train_x.shape[0]
    sum_specs = [pl.BlockSpec((TILE, HD), lambda i, p: (i, 0)), vmem((VSEQ, HD))]
    first = sums is None
    picks = extra or n
    pick_spec = pl.BlockSpec((picks, TILE, NY * ROWS), lambda i, p: (0, i, 0))
    return call(
        functools.partial(project_kernel, n, extra, first),
        (where,),
        (*[train_x] * (n + extra), *[val_x] * n, *weights, *([] if first else sums)),
        waits,
        (rows // TILE,),
        [pl.BlockSpec((TILE, WIDE), lambda i, p, dz=dz: (i, z_of(p, dz))) for dz in (*zs, *others)]
        + [pl.BlockSpec((VSEQ, WIDE), lambda i, p, dz=dz: (0, z_of(p, dz))) for dz in zs]
        + [vmem((NC * NY, ROWS, HD))] * n
        + ([] if first else sum_specs),
        sum_specs + [pick_spec],
        [
            jax.ShapeDtypeStruct((rows, HD), f32),
            jax.ShapeDtypeStruct((VSEQ, HD), f32),
            jax.ShapeDtypeStruct((picks, rows, NY * ROWS), bf16),
        ],
        cost(2 * rows * n * WIDE * HD, 2 * rows * n * WIDE),
        [pltpu.VMEM((WIDE, HD), bf16)] * n,
    )


def grads_kernel(place_ref, x_ref, w_ref, sum_ref, p_ref, target_ref, out_ref, whole):
    @pl.when(pl.program_id(0) == 0)
    def _():
        lay_weights(place_ref, w_ref, whole)

    values = (sum_ref[...] + dot(x_ref[...], whole[...])).astype(bf16)
    attention = p_ref[0].reshape(GROUP * SEQ, SEQ)
    mixed = dot(attention, values)
    target = jnp.concatenate(
        [target_ref[:, h * HD : (h + 1) * HD] for h in range(GROUP)], axis=0
    ).astype(f32)
    residual = ((mixed - target) * (1.0 / SEQ)).astype(bf16)
    pulled = dot(residual, attention, ((0,), (0,)))
    out_ref[...] = pulled.astype(bf16)


def value_grads(where, train_x, weights, sums, attention, target, waits=()):
    rows = train_x.shape[0]
    return call(
        grads_kernel,
        (where,),
        (train_x, weights, sums, attention, target),
        waits,
        (MEMBERS,),
        [
            pl.BlockSpec((SEQ, WIDE), lambda i, p: (i, z_of(p, 4))),
            vmem((NC * NY, ROWS, HD)),
            pl.BlockSpec((SEQ, HD), lambda i, p: (i, 0)),
            pl.BlockSpec((1, GROUP, SEQ, SEQ), lambda i, p: (i, 0, 0, 0)),
            pl.BlockSpec((SEQ, GROUP * HD), lambda i, p: (i, 0)),
        ],
        pl.BlockSpec((HD, SEQ), lambda i, p: (0, i)),
        jax.ShapeDtypeStruct((HD, rows), bf16),
        cost(4 * rows * GROUP * SEQ * HD, 8 * 2**20),
        [pltpu.VMEM((WIDE, HD), bf16)],
    )


def val_kernel(place_ref, x_ref, w_ref, sum_ref, p_ref, target_ref, out_ref, whole):
    lay_weights(place_ref, w_ref, whole)
    values = (sum_ref[...] + dot(x_ref[...], whole[...])).astype(bf16)
    attention = p_ref[0].reshape(GROUP * VSEQ, VSEQ)
    target = jnp.concatenate(
        [target_ref[:, h * HD : (h + 1) * HD] for h in range(GROUP)], axis=0
    ).astype(f32)
    residual = (dot(attention, values) - target) * (1.0 / VSEQ)
    high = residual.astype(bf16)
    low = (residual - high.astype(f32)).astype(bf16)
    pulled = dot(high, attention, ((0,), (0,))) + dot(low, attention, ((0,), (0,)))
    out_ref[...] = pulled.astype(bf16)


def val_pulls(where, val_x, weights, sums, attention, target, waits=()):
    return call(
        val_kernel,
        (where,),
        (val_x, weights, sums, attention, target),
        waits,
        (1,),
        [
            pl.BlockSpec((VSEQ, WIDE), lambda i, p: (0, z_of(p, 4))),
            vmem((NC * NY, ROWS, HD)),
            vmem((VSEQ, HD)),
            vmem((1, GROUP, VSEQ, VSEQ)),
            vmem((VSEQ, GROUP * HD)),
        ],
        vmem((HD, VSEQ)),
        jax.ShapeDtypeStruct((HD, VSEQ), bf16),
        cost(10 * VSEQ * GROUP * VSEQ * HD, 2**20),
        [pltpu.VMEM((WIDE, HD), bf16)],
    )


def skills_kernel(place_ref, own_x, other_x, own_grads, other_grads, out_ref, total):
    total[...] = jnp.zeros_like(total)
    for k, (x_ref, grads_ref) in enumerate(((own_x, own_grads), (other_x.at[0], other_grads))):
        for m in range(MEMBERS):
            tokens = slice(m * SEQ, (m + 1) * SEQ)
            total[place_ref[3 + k * MEMBERS + m]] += dot(grads_ref[:, tokens], x_ref[tokens, :])
    out_ref[0, 0] = total[...].reshape(SKILLS * HD, ROWS)


def skill_terms(where, own_x, other_x, grads, zs, waits=()):
    rows = own_x.shape[0]
    first, step = zs[0], zs[-1] - zs[0]

    def pair_of(i, j, p):
        return z_of(p, first + i * step) * 2 + lax.rem(p[1] + j, NY)

    return call(
        skills_kernel,
        (where,),
        (own_x, other_x, *grads),
        waits,
        (len(zs), NY),
        [
            pl.BlockSpec((rows, ROWS), lambda i, j, p: (0, pair_of(i, j, p) * 2 + p[2])),
            pl.BlockSpec((1, rows, ROWS), lambda i, j, p: (i, 0, lax.rem(p[1] + j, NY))),
            pl.BlockSpec((HD, rows), lambda i, j, p: (0, 0)),
            pl.BlockSpec((HD, rows), lambda i, j, p: (0, 0)),
        ],
        pl.BlockSpec((1, 1, SKILLS * HD, ROWS), lambda i, j, p: (i, j, 0, 0)),
        jax.ShapeDtypeStruct((len(zs), NY, SKILLS * HD, ROWS), f32),
        cost(2 * rows * len(zs) * WIDE * HD, len(zs) * 5 * 2**20),
        [pltpu.VMEM((SKILLS, HD, ROWS), f32)],
    )


HALF = SKILLS * HD


def step_kernel(step, mine_ref, up_ref, down_ref, up_out, down_out):
    if step == 1:
        up_out[:HALF, :] = mine_ref[0, 0].astype(bf16)
        down_out[:HALF, :] = mine_ref[0, 1].astype(bf16)
        up_out[HALF:, :] = up_ref[...]
        down_out[HALF:, :] = down_ref[...]
        return
    for dy in range(NY):
        rows = slice(dy * HALF, (dy + 1) * HALF)
        if step == 2:
            came = (up_ref if dy == 0 else None, down_ref if dy == 1 else None)
            there = slice(0, HALF)
        else:
            came, there = (up_ref, down_ref), rows
        for k, (ref, out) in enumerate(zip(came, (up_out, down_out))):
            total = mine_ref[k, dy]
            if ref is not None:
                total = total + ref[there, :].astype(f32)
            out[rows, :] = total.astype(bf16)
    if step < 4:
        for ref, out in ((up_ref, up_out), (down_ref, down_out)):
            out[NY * HALF :, :] = ref[ref.shape[0] - HD :, :]


def ring_step(step, mine, up, down):
    rows = {1: HALF + HD, 2: NY * HALF + HD, 3: NY * HALF + HD, 4: NY * HALF}[step]
    shape = (rows, ROWS)
    operands = (mine, up, down)
    up, down = call(
        functools.partial(step_kernel, step),
        (),
        operands,
        (),
        (1,),
        [vmem(o.shape) for o in operands],
        [vmem(shape), vmem(shape)],
        [jax.ShapeDtypeStruct(shape, bf16)] * 2,
        cost(2**20, 4 * 2**20),
        mib=16,
    )
    return up, (send(up, UP), send(down, DOWN))


def stack_kernel(*refs):
    for i, ref in enumerate(refs[:-1]):
        refs[-1][i] = ref[...]


def stacked(arrays, waits=()):
    tails = [pl.BlockSpec((HD, ROWS), lambda i, n=a.shape[0] // HD - 1: (n, 0)) for a in arrays]
    return call(
        stack_kernel,
        (),
        arrays,
        waits,
        (1,),
        tails,
        vmem((len(arrays), HD, ROWS)),
        jax.ShapeDtypeStruct((len(arrays), HD, ROWS), bf16),
        cost(0, 2**20),
        mib=16,
    )


def copies_kernel(from_ref, to_ref):
    to_ref[0] = from_ref[...]


def copies(array, count, waits):
    return call(
        copies_kernel,
        (),
        (array,),
        waits,
        (count,),
        [vmem(array.shape)],
        pl.BlockSpec((1,) + array.shape, lambda i: (i, 0, 0, 0)),
        jax.ShapeDtypeStruct((count,) + array.shape, array.dtype),
        cost(0, 2**20),
        mib=16,
    )


def directions_kernel(place_ref, skill_ref, near_ref, far_ref, x_ref, out_ref):
    out_ref[...] = jnp.zeros_like(out_ref)
    for dz in range(NZ):
        for dy in range(NY):
            for dc, ref in enumerate((near_ref, far_ref)):
                f = z_of(place_ref, dz) * 4 + lax.rem(place_ref[1] + dy, NY) * 2 + lax.rem(place_ref[2] + dc, NC)
                tokens = x_ref[:, f].reshape(VSEQ, ROWS)
                out_ref[skill_ref[f]] += dot(ref[dz, :, dy * HD : (dy + 1) * HD], tokens)


def directions_of(where, val_skill, near, far, columns):
    return call(
        directions_kernel,
        (where, val_skill),
        (near, far, columns),
        (),
        (1,),
        [vmem(near.shape), vmem(far.shape), vmem(columns.shape)],
        vmem((SKILLS, HD, ROWS)),
        jax.ShapeDtypeStruct((SKILLS, HD, ROWS), f32),
        cost(2 * 4096 * ROWS * HD, 4 * 2**20),
        mib=16,
    )


EVERY = NZ * NY * NC * NX * NL


def local_kernel(mine_ref, up_ref, down_ref, here_ref, there_ref, keep_ref, give_ref, local_ref):
    lane = lax.broadcasted_iota(jnp.int32, (1, HD), 1)
    local = jnp.zeros((1, HD), f32)
    for s in range(SKILLS):
        rows = slice(s * HD, (s + 1) * HD)
        totals = [
            mine_ref[0, dy, rows, :]
            + up_ref[dy * HALF + s * HD : dy * HALF + (s + 1) * HD, :].astype(f32)
            + down_ref[dy * HALF + s * HD : dy * HALF + (s + 1) * HD, :].astype(f32)
            for dy in range(NY)
        ]
        keep_ref[rows, :] = totals[0]
        give_ref[rows, :] = totals[1].astype(bf16)
        for v in range(SKILLS):
            product = totals[0] * here_ref[v] + totals[1] * there_ref[v].astype(f32)
            product = jnp.sum(product, axis=0, keepdims=True)
            entry = step_size * jnp.sum(product, axis=1, keepdims=True)
            local = jnp.where(lane == s * SKILLS + v, entry, local)
    local_ref[...] = jnp.broadcast_to(local, local_ref.shape)


def local_transfer(mine, up, down, here, there):
    operands = (mine, up, down, here, there)
    return call(
        local_kernel,
        (),
        operands,
        (),
        (1,),
        [vmem(o.shape) for o in operands],
        [vmem((SKILLS * HD, ROWS)), vmem((SKILLS * HD, ROWS)), vmem((EVERY, 1, HD))],
        [
            jax.ShapeDtypeStruct((SKILLS * HD, ROWS), f32),
            jax.ShapeDtypeStruct((SKILLS * HD, ROWS), bf16),
            jax.ShapeDtypeStruct((EVERY, 1, HD), f32),
        ],
        cost(2**22, 4 * 2**20),
        mib=16,
    )


def finish_kernel(keep_ref, got_ref, grads_ref):
    for s in range(SKILLS):
        rows = slice(s * HD, (s + 1) * HD)
        grads_ref[s] = (keep_ref[rows, :] + got_ref[rows, :].astype(f32)).T.astype(bf16)


def finish(keep, got):
    return call(
        finish_kernel,
        (),
        (keep, got),
        (),
        (1,),
        [vmem(keep.shape), vmem(got.shape)],
        vmem((SKILLS, ROWS, HD)),
        jax.ShapeDtypeStruct((SKILLS, ROWS, HD), bf16),
        cost(2**20, 2**20),
        mib=16,
    )


def rows_kernel(rows_ref, out_ref):
    row = jnp.sum(rows_ref[...], axis=0)
    for s in range(SKILLS):
        out_ref[s : s + 1, :] = row[:, s * SKILLS : (s + 1) * SKILLS]


def sum_rows(rows, waits):
    return call(
        rows_kernel,
        (),
        (rows,),
        waits,
        (1,),
        [vmem(rows.shape)],
        vmem((SKILLS, SKILLS)),
        jax.ShapeDtypeStruct((SKILLS, SKILLS), f32),
        cost(2**20, 2**20),
        mib=16,
    )


def on_device(
    train_x, train_q, train_k, train_target, train_skill, value_weight, val_x, val_q, val_k, val_target, val_skill
):
    f, t = lax.axis_index("fsdp"), lax.axis_index("tp")
    z, y, c = f // 4, (f // 2) % 2, f % 2
    own_skill = lax.dynamic_slice_in_dim(train_skill, f * MEMBERS, MEMBERS)
    other_skill = lax.dynamic_slice_in_dim(train_skill, (f + 1 - 2 * c) * MEMBERS, MEMBERS)
    where = jnp.concatenate([jnp.stack([z, y, c]).astype(jnp.int32), own_skill, other_skill])

    part = VSEQ // 8
    own_tokens = lax.dynamic_slice_in_dim(val_x, t * part, part).reshape(part, 32, ROWS)
    crossed = lax.all_to_all(own_tokens.transpose(1, 0, 2), "fsdp", 0, 0)

    own = value_weight
    quad = jnp.stack([own, send(own, YHI), send(own, CORE), send(own, DIAGONAL)])
    val_attention = attend(val_q, val_k, VSEQ)
    attention = attend(train_q, train_k, SEQ, (val_attention, quad))
    up1, down1 = send(quad, UP), send(quad, DOWN)
    up1, down1 = joined((up1, down1), (attention,))
    up2, down2 = send(up1, UP), send(down1, DOWN)
    *sums, picked = project(where, train_x, val_x, (0,), [quad], None, (attention, up1, crossed), (4, 0))
    other_x = {(4,): send(picked[:1], CORE), (0,): send(picked[1:], CORE)}
    up2, down2 = joined((up2, down2), (sums[1],))
    up3, down3 = send(up2, UP), send(down2, DOWN)
    *sums, picked = project(where, train_x, val_x, (1, 7), [down1, up1], sums)
    other_x[1, 7] = send(picked, CORE)
    up3, down3 = joined((up3, down3), (sums[1],))
    last = jnp.concatenate([send(up3[:2], UP), send(down3[2:], DOWN)])
    *sums, picked = project(where, train_x, val_x, (2, 6), [down2, up2], sums)
    *sums, later = project(where, train_x, val_x, (3, 5), [down3, up3], sums)
    own_pull = val_pulls(where, val_x, last, sums[1], val_attention, val_target)
    other_x[3, 5] = send(joined((later,), (own_pull,))[0], CORE)
    pull = jnp.concatenate([own_pull, send(own_pull, YHI)], axis=1)
    p_up, p_down = send(pull, UP), send(pull, DOWN)
    grads = value_grads(where, train_x, last, sums[0], attention, train_target, (own_pull,))
    grads = (grads, send(grads, CORE))

    def terms(zs, *waits):
        return skill_terms(where, train_x, other_x[zs], grads, zs, waits)

    pulls = {0: pull, 1: p_down, 7: p_up}
    sent, (up, down) = ring_step(1, terms((4,)), p_up, p_down)
    mine = terms((3, 5), sent)
    other_x[2, 6] = send(joined((picked,), (sent,))[0], CORE)
    columns = lax.all_to_all(copies(crossed, NX * NL, (sent,)), "tp", 0, 0)
    pulls[6], pulls[2] = up, down
    sent, (up, down) = ring_step(2, mine, up, down)
    mine = terms((2, 6), sent)
    pulls[5], pulls[3] = up, down
    sent, (up, down) = ring_step(3, mine, up, down)
    mine = terms((1, 7), sent)
    pulls[4] = up
    sent, (up, down) = ring_step(4, mine, up, down)
    near_pulls = stacked([pulls[dz] for dz in range(NZ)], (sent,))
    here = directions_of(where, val_skill, near_pulls, send(near_pulls, CORE), columns)
    there = send(here.astype(bf16), YHI)
    keep, give, local = local_transfer(terms((0,), sent, here), up, down, here, there)
    rows = lax.all_to_all(local, ("fsdp", "tp"), 0, 0)
    skill_grads = finish(keep, send(give, YHI))
    return (skill_grads, sum_rows(rows, (skill_grads,)))


def solution(mesh):
    placed = (
        P("fsdp", None),
        P("fsdp", "tp"),
        P("fsdp", "tp"),
        P("fsdp", "tp"),
        P(),
        P("fsdp", "tp"),
        P("fsdp", None),
        P("fsdp", "tp"),
        P("fsdp", "tp"),
        P("fsdp", "tp"),
        P(),
    )
    return jax.shard_map(
        on_device,
        mesh=mesh,
        in_specs=placed,
        out_specs=(P(None, "fsdp", "tp"), P()),
        check_vma=False,
    )
```

```python
import functools
import math

import jax
import jax.numpy as jnp
from jax import lax
from jax.experimental import pallas as pl
from jax.experimental.pallas import tpu as pltpu
from jax.sharding import PartitionSpec as P

HD = 128
GROUP = 8
SKILLS = 4
SEQ = 256
VSEQ = 128
MEMBERS = 4
NZ, NY, NC = 8, 2, 2
NX, NL = 4, 2
ROWS = 256

step_size = 0.01
bf16 = jnp.bfloat16
f32 = jnp.float32


def place(z, y, c):
    return (z % NZ) * 4 + (y % NY) * 2 + (c % NC)


def moves(fn):
    return [
        (place(z, y, c), place(*fn(z, y, c)))
        for z in range(NZ)
        for y in range(NY)
        for c in range(NC)
    ]


DIAGONAL = moves(lambda z, y, c: (z, y + 1, c + 1))
CORE = moves(lambda z, y, c: (z, y, c + 1))
YHI = moves(lambda z, y, c: (z, y + 1, c))
UP = moves(lambda z, y, c: (z + 1, y, c))
DOWN = moves(lambda z, y, c: (z - 1, y, c))


def send(value, way):
    return lax.ppermute(value, "fsdp", way)


def call(kernel, prefetched, operands, waits, grid, in_specs, out_specs, out_shape, cost_estimate, scratch=(), mib=50):
    first = len(prefetched) + len(operands)

    def body(*refs):
        kernel(*refs[:first], *refs[first + len(waits) :])

    return pl.pallas_call(
        body,
        grid_spec=pltpu.PrefetchScalarGridSpec(
            num_scalar_prefetch=len(prefetched),
            grid=grid,
            in_specs=list(in_specs) + [pl.BlockSpec(memory_space=pl.ANY)] * len(waits),
            out_specs=out_specs,
            scratch_shapes=list(scratch),
        ),
        out_shape=out_shape,
        compiler_params=pltpu.CompilerParams(vmem_limit_bytes=mib * 2**20),
        cost_estimate=cost_estimate,
    )(*prefetched, *operands, *waits)


def joined(values, waits):
    return pl.pallas_call(
        lambda *refs: None,
        in_specs=[pl.BlockSpec(memory_space=pl.ANY)] * (len(values) + len(waits)),
        out_specs=[pl.BlockSpec(memory_space=pl.ANY)] * len(values),
        out_shape=[jax.ShapeDtypeStruct(v.shape, v.dtype) for v in values],
        input_output_aliases={i: i for i in range(len(values))},
        compiler_params=pltpu.CompilerParams(vmem_limit_bytes=50 * 2**20),
        cost_estimate=cost(1, 1),
    )(*values, *waits)


def vmem(shape):
    return pl.BlockSpec(shape, lambda i, *_: (0,) * len(shape))


def cost(flops, moved, exps=0):
    return pl.CostEstimate(flops=flops // 4096, bytes_accessed=moved // 4096, transcendentals=exps // 4096)


def dot(a, b, dims=((1,), (0,))):
    return lax.dot_general(a, b, (dims, ((), ())), preferred_element_type=f32)


def attend_kernel(length, q_ref, k_ref, p_ref):
    keys = k_ref[...]
    rows = lax.broadcasted_iota(jnp.int32, (length, length), 0)
    columns = lax.broadcasted_iota(jnp.int32, (length, length), 1)
    allowed = rows >= columns
    for h in range(GROUP):
        scores = dot(q_ref[:, h * HD : (h + 1) * HD], keys, ((1,), (1,)))
        scores = jnp.where(allowed, scores * (1.0 / math.sqrt(HD)), jnp.float32(-1e30))
        raised = jnp.exp(scores - jnp.max(scores, axis=-1, keepdims=True))
        total = jnp.sum(raised, axis=-1, keepdims=True)
        p_ref[0, h] = (raised * (1.0 / total)).astype(bf16)


def attend(queries, keys, length, waits=()):
    members = queries.shape[0] // length
    count = members * GROUP * length * length
    return call(
        functools.partial(attend_kernel, length),
        (),
        (queries, keys),
        waits,
        (members,),
        [
            pl.BlockSpec((length, GROUP * HD), lambda i: (i, 0)),
            pl.BlockSpec((length, HD), lambda i: (i, 0)),
        ],
        pl.BlockSpec((1, GROUP, length, length), lambda i: (i, 0, 0, 0)),
        jax.ShapeDtypeStruct((members, GROUP, length, length), bf16),
        cost(2 * count * HD, 4 * count, count),
    )


def z_of(place_ref, dz):
    return lax.rem(place_ref[0] + dz, NZ)


def lay_weights(place_ref, blocks, whole):
    for dc in range(NC):
        for dy in range(NY):
            y = lax.rem(place_ref[1] + dy, NY)
            c = lax.rem(place_ref[2] + dc, NC)
            row = pl.multiple_of((y * 2 + c) * ROWS, ROWS)
            whole[pl.ds(row, ROWS), :] = blocks[dc * NY + dy]


def project_kernel(n, extra, first, place_ref, *refs):
    xs, refs = refs[: n + extra], refs[n + extra :]
    vs, refs = refs[:n], refs[n:]
    ws, refs = refs[:n], refs[n:]
    if first:
        sum_out, val_out, pick_out, *whole = refs
    else:
        sum_in, val_in, sum_out, val_out, pick_out, *whole = refs

    @pl.when(pl.program_id(0) == 0)
    def _():
        for j in range(n):
            lay_weights(place_ref, ws[j], whole[j])
        total = sum(dot(vs[j][...], whole[j][...]) for j in range(n))
        val_out[...] = total if first else total + val_in[...]

    total = sum(dot(xs[j][...], whole[j][...]) for j in range(n))
    sum_out[...] = total if first else total + sum_in[...]
    for j, x_ref in enumerate(xs[n if extra else 0 :]):
        for y in range(NY):
            column = pl.multiple_of((y * 2 + 1 - place_ref[2]) * ROWS, ROWS)
            pick_out[j, :, y * ROWS : (y + 1) * ROWS] = x_ref[:, pl.ds(column, ROWS)]


WIDE = NY * NC * ROWS
TILE = 512


def project(where, train_x, val_x, zs, weights, sums, waits=(), others=()):
    n, extra = len(zs), len(others)
    rows = train_x.shape[0]
    sum_specs = [pl.BlockSpec((TILE, HD), lambda i, p: (i, 0)), vmem((VSEQ, HD))]
    first = sums is None
    picks = extra or n
    pick_spec = pl.BlockSpec((picks, TILE, NY * ROWS), lambda i, p: (0, i, 0))
    return call(
        functools.partial(project_kernel, n, extra, first),
        (where,),
        (*[train_x] * (n + extra), *[val_x] * n, *weights, *([] if first else sums)),
        waits,
        (rows // TILE,),
        [pl.BlockSpec((TILE, WIDE), lambda i, p, dz=dz: (i, z_of(p, dz))) for dz in (*zs, *others)]
        + [pl.BlockSpec((VSEQ, WIDE), lambda i, p, dz=dz: (0, z_of(p, dz))) for dz in zs]
        + [vmem((NC * NY, ROWS, HD))] * n
        + ([] if first else sum_specs),
        sum_specs + [pick_spec],
        [
            jax.ShapeDtypeStruct((rows, HD), f32),
            jax.ShapeDtypeStruct((VSEQ, HD), f32),
            jax.ShapeDtypeStruct((picks, rows, NY * ROWS), bf16),
        ],
        cost(2 * rows * n * WIDE * HD, 2 * rows * n * WIDE),
        [pltpu.VMEM((WIDE, HD), bf16)] * n,
    )


def grads_kernel(place_ref, x_ref, w_ref, sum_ref, p_ref, target_ref, out_ref, whole):
    @pl.when(pl.program_id(0) == 0)
    def _():
        lay_weights(place_ref, w_ref, whole)

    values = (sum_ref[...] + dot(x_ref[...], whole[...])).astype(bf16)
    attention = p_ref[0].reshape(GROUP * SEQ, SEQ)
    mixed = dot(attention, values)
    target = jnp.concatenate(
        [target_ref[:, h * HD : (h + 1) * HD] for h in range(GROUP)], axis=0
    ).astype(f32)
    residual = ((mixed - target) * (1.0 / SEQ)).astype(bf16)
    pulled = dot(residual, attention, ((0,), (0,)))
    out_ref[...] = pulled.astype(bf16)


def value_grads(where, train_x, weights, sums, attention, target, waits=()):
    rows = train_x.shape[0]
    return call(
        grads_kernel,
        (where,),
        (train_x, weights, sums, attention, target),
        waits,
        (MEMBERS,),
        [
            pl.BlockSpec((SEQ, WIDE), lambda i, p: (i, z_of(p, 4))),
            vmem((NC * NY, ROWS, HD)),
            pl.BlockSpec((SEQ, HD), lambda i, p: (i, 0)),
            pl.BlockSpec((1, GROUP, SEQ, SEQ), lambda i, p: (i, 0, 0, 0)),
            pl.BlockSpec((SEQ, GROUP * HD), lambda i, p: (i, 0)),
        ],
        pl.BlockSpec((HD, SEQ), lambda i, p: (0, i)),
        jax.ShapeDtypeStruct((HD, rows), bf16),
        cost(4 * rows * GROUP * SEQ * HD, 8 * 2**20),
        [pltpu.VMEM((WIDE, HD), bf16)],
    )


def val_kernel(place_ref, x_ref, w_ref, sum_ref, p_ref, target_ref, out_ref, whole):
    lay_weights(place_ref, w_ref, whole)
    values = (sum_ref[...] + dot(x_ref[...], whole[...])).astype(bf16)
    attention = p_ref[0].reshape(GROUP * VSEQ, VSEQ)
    target = jnp.concatenate(
        [target_ref[:, h * HD : (h + 1) * HD] for h in range(GROUP)], axis=0
    ).astype(f32)
    residual = (dot(attention, values) - target) * (1.0 / VSEQ)
    high = residual.astype(bf16)
    low = (residual - high.astype(f32)).astype(bf16)
    pulled = dot(high, attention, ((0,), (0,))) + dot(low, attention, ((0,), (0,)))
    out_ref[...] = pulled.astype(bf16)


def val_pulls(where, val_x, weights, sums, attention, target, waits=()):
    return call(
        val_kernel,
        (where,),
        (val_x, weights, sums, attention, target),
        waits,
        (1,),
        [
            pl.BlockSpec((VSEQ, WIDE), lambda i, p: (0, z_of(p, 4))),
            vmem((NC * NY, ROWS, HD)),
            vmem((VSEQ, HD)),
            vmem((1, GROUP, VSEQ, VSEQ)),
            vmem((VSEQ, GROUP * HD)),
        ],
        vmem((HD, VSEQ)),
        jax.ShapeDtypeStruct((HD, VSEQ), bf16),
        cost(10 * VSEQ * GROUP * VSEQ * HD, 2**20),
        [pltpu.VMEM((WIDE, HD), bf16)],
    )


def skills_kernel(place_ref, own_x, other_x, own_grads, other_grads, out_ref, total):
    total[...] = jnp.zeros_like(total)
    for k, (x_ref, grads_ref) in enumerate(((own_x, own_grads), (other_x.at[0], other_grads))):
        for m in range(MEMBERS):
            tokens = slice(m * SEQ, (m + 1) * SEQ)
            total[place_ref[3 + k * MEMBERS + m]] += dot(grads_ref[:, tokens], x_ref[tokens, :])
    out_ref[0, 0] = total[...].reshape(SKILLS * HD, ROWS)


def skill_terms(where, own_x, other_x, grads, zs, waits=()):
    rows = own_x.shape[0]
    first, step = zs[0], zs[-1] - zs[0]

    def pair_of(i, j, p):
        return z_of(p, first + i * step) * 2 + lax.rem(p[1] + j, NY)

    return call(
        skills_kernel,
        (where,),
        (own_x, other_x, *grads),
        waits,
        (len(zs), NY),
        [
            pl.BlockSpec((rows, ROWS), lambda i, j, p: (0, pair_of(i, j, p) * 2 + p[2])),
            pl.BlockSpec((1, rows, ROWS), lambda i, j, p: (i, 0, lax.rem(p[1] + j, NY))),
            pl.BlockSpec((HD, rows), lambda i, j, p: (0, 0)),
            pl.BlockSpec((HD, rows), lambda i, j, p: (0, 0)),
        ],
        pl.BlockSpec((1, 1, SKILLS * HD, ROWS), lambda i, j, p: (i, j, 0, 0)),
        jax.ShapeDtypeStruct((len(zs), NY, SKILLS * HD, ROWS), f32),
        cost(2 * rows * len(zs) * WIDE * HD, len(zs) * 5 * 2**20),
        [pltpu.VMEM((SKILLS, HD, ROWS), f32)],
    )


HALF = SKILLS * HD


def step_kernel(step, mine_ref, up_ref, down_ref, up_out, down_out):
    if step == 1:
        up_out[:HALF, :] = mine_ref[0, 0].astype(bf16)
        down_out[:HALF, :] = mine_ref[0, 1].astype(bf16)
        up_out[HALF:, :] = up_ref[...]
        down_out[HALF:, :] = down_ref[...]
        return
    for dy in range(NY):
        rows = slice(dy * HALF, (dy + 1) * HALF)
        if step == 2:
            came = (up_ref if dy == 0 else None, down_ref if dy == 1 else None)
            there = slice(0, HALF)
        else:
            came, there = (up_ref, down_ref), rows
        for k, (ref, out) in enumerate(zip(came, (up_out, down_out))):
            total = mine_ref[k, dy]
            if ref is not None:
                total = total + ref[there, :].astype(f32)
            out[rows, :] = total.astype(bf16)
    if step < 4:
        for ref, out in ((up_ref, up_out), (down_ref, down_out)):
            out[NY * HALF :, :] = ref[ref.shape[0] - HD :, :]


def ring_step(step, mine, up, down):
    rows = {1: HALF + HD, 2: NY * HALF + HD, 3: NY * HALF + HD, 4: NY * HALF}[step]
    shape = (rows, ROWS)
    operands = (mine, up, down)
    up, down = call(
        functools.partial(step_kernel, step),
        (),
        operands,
        (),
        (1,),
        [vmem(o.shape) for o in operands],
        [vmem(shape), vmem(shape)],
        [jax.ShapeDtypeStruct(shape, bf16)] * 2,
        cost(2**20, 4 * 2**20),
        mib=16,
    )
    return up, (send(up, UP), send(down, DOWN))


def stack_kernel(*refs):
    for i, ref in enumerate(refs[:-1]):
        refs[-1][i] = ref[...]


def stacked(arrays, waits=()):
    tails = [pl.BlockSpec((HD, ROWS), lambda i, n=a.shape[0] // HD - 1: (n, 0)) for a in arrays]
    return call(
        stack_kernel,
        (),
        arrays,
        waits,
        (1,),
        tails,
        vmem((len(arrays), HD, ROWS)),
        jax.ShapeDtypeStruct((len(arrays), HD, ROWS), bf16),
        cost(0, 2**20),
        mib=16,
    )


def copies_kernel(from_ref, to_ref):
    to_ref[0] = from_ref[...]


def copies(array, count, waits):
    return call(
        copies_kernel,
        (),
        (array,),
        waits,
        (count,),
        [vmem(array.shape)],
        pl.BlockSpec((1,) + array.shape, lambda i: (i, 0, 0, 0)),
        jax.ShapeDtypeStruct((count,) + array.shape, array.dtype),
        cost(0, 2**20),
        mib=16,
    )


def directions_kernel(place_ref, skill_ref, near_ref, far_ref, x_ref, out_ref):
    out_ref[...] = jnp.zeros_like(out_ref)
    for dz in range(NZ):
        for dy in range(NY):
            for dc, ref in enumerate((near_ref, far_ref)):
                f = z_of(place_ref, dz) * 4 + lax.rem(place_ref[1] + dy, NY) * 2 + lax.rem(place_ref[2] + dc, NC)
                tokens = x_ref[:, f].reshape(VSEQ, ROWS)
                out_ref[skill_ref[f]] += dot(ref[dz, :, dy * HD : (dy + 1) * HD], tokens)


def directions_of(where, val_skill, near, far, columns):
    return call(
        directions_kernel,
        (where, val_skill),
        (near, far, columns),
        (),
        (1,),
        [vmem(near.shape), vmem(far.shape), vmem(columns.shape)],
        vmem((SKILLS, HD, ROWS)),
        jax.ShapeDtypeStruct((SKILLS, HD, ROWS), f32),
        cost(2 * 4096 * ROWS * HD, 4 * 2**20),
        mib=16,
    )


EVERY = NZ * NY * NC * NX * NL


def local_kernel(mine_ref, up_ref, down_ref, here_ref, there_ref, keep_ref, give_ref, local_ref):
    lane = lax.broadcasted_iota(jnp.int32, (1, HD), 1)
    local = jnp.zeros((1, HD), f32)
    for s in range(SKILLS):
        rows = slice(s * HD, (s + 1) * HD)
        totals = [
            mine_ref[0, dy, rows, :]
            + up_ref[dy * HALF + s * HD : dy * HALF + (s + 1) * HD, :].astype(f32)
            + down_ref[dy * HALF + s * HD : dy * HALF + (s + 1) * HD, :].astype(f32)
            for dy in range(NY)
        ]
        keep_ref[rows, :] = totals[0]
        give_ref[rows, :] = totals[1].astype(bf16)
        for v in range(SKILLS):
            product = totals[0] * here_ref[v] + totals[1] * there_ref[v].astype(f32)
            product = jnp.sum(product, axis=0, keepdims=True)
            entry = step_size * jnp.sum(product, axis=1, keepdims=True)
            local = jnp.where(lane == s * SKILLS + v, entry, local)
    local_ref[...] = jnp.broadcast_to(local, local_ref.shape)


def local_transfer(mine, up, down, here, there):
    operands = (mine, up, down, here, there)
    return call(
        local_kernel,
        (),
        operands,
        (),
        (1,),
        [vmem(o.shape) for o in operands],
        [vmem((SKILLS * HD, ROWS)), vmem((SKILLS * HD, ROWS)), vmem((EVERY, 1, HD))],
        [
            jax.ShapeDtypeStruct((SKILLS * HD, ROWS), f32),
            jax.ShapeDtypeStruct((SKILLS * HD, ROWS), bf16),
            jax.ShapeDtypeStruct((EVERY, 1, HD), f32),
        ],
        cost(2**22, 4 * 2**20),
        mib=16,
    )


def finish_kernel(keep_ref, got_ref, grads_ref):
    for s in range(SKILLS):
        rows = slice(s * HD, (s + 1) * HD)
        grads_ref[s] = (keep_ref[rows, :] + got_ref[rows, :].astype(f32)).T.astype(bf16)


def finish(keep, got):
    return call(
        finish_kernel,
        (),
        (keep, got),
        (),
        (1,),
        [vmem(keep.shape), vmem(got.shape)],
        vmem((SKILLS, ROWS, HD)),
        jax.ShapeDtypeStruct((SKILLS, ROWS, HD), bf16),
        cost(2**20, 2**20),
        mib=16,
    )


def rows_kernel(rows_ref, out_ref):
    row = jnp.sum(rows_ref[...], axis=0)
    for s in range(SKILLS):
        out_ref[s : s + 1, :] = row[:, s * SKILLS : (s + 1) * SKILLS]


def sum_rows(rows, waits):
    return call(
        rows_kernel,
        (),
        (rows,),
        waits,
        (1,),
        [vmem(rows.shape)],
        vmem((SKILLS, SKILLS)),
        jax.ShapeDtypeStruct((SKILLS, SKILLS), f32),
        cost(2**20, 2**20),
        mib=16,
    )


def on_device(
    train_x, train_q, train_k, train_target, train_skill, value_weight, val_x, val_q, val_k, val_target, val_skill
):
    f, t = lax.axis_index("fsdp"), lax.axis_index("tp")
    z, y, c = f // 4, (f // 2) % 2, f % 2
    own_skill = lax.dynamic_slice_in_dim(train_skill, f * MEMBERS, MEMBERS)
    other_skill = lax.dynamic_slice_in_dim(train_skill, (f + 1 - 2 * c) * MEMBERS, MEMBERS)
    where = jnp.concatenate([jnp.stack([z, y, c]).astype(jnp.int32), own_skill, other_skill])

    part = VSEQ // 8
    own_tokens = lax.dynamic_slice_in_dim(val_x, t * part, part).reshape(part, 32, ROWS)
    crossed = lax.all_to_all(own_tokens.transpose(1, 0, 2), "fsdp", 0, 0)

    own = value_weight
    quad = jnp.stack([own, send(own, YHI), send(own, CORE), send(own, DIAGONAL)])
    val_attention = attend(val_q, val_k, VSEQ)
    attention = attend(train_q, train_k, SEQ, (val_attention, quad))
    up1, down1 = send(quad, UP), send(quad, DOWN)
    up1, down1 = joined((up1, down1), (attention,))
    up2, down2 = send(up1, UP), send(down1, DOWN)
    *sums, picked = project(where, train_x, val_x, (0,), [quad], None, (attention, up1, crossed), (4, 0))
    other_x = {(4,): send(picked[:1], CORE), (0,): send(picked[1:], CORE)}
    up2, down2 = joined((up2, down2), (sums[1],))
    up3, down3 = send(up2, UP), send(down2, DOWN)
    *sums, picked = project(where, train_x, val_x, (1, 7), [down1, up1], sums)
    other_x[1, 7] = send(picked, CORE)
    up3, down3 = joined((up3, down3), (sums[1],))
    last = jnp.concatenate([send(up3[:2], UP), send(down3[2:], DOWN)])
    *sums, picked = project(where, train_x, val_x, (3, 5), [down3, up3], sums)
    other_x[3, 5] = send(picked, CORE)
    *sums, picked = project(where, train_x, val_x, (2, 6), [down2, up2], sums)
    own_pull = val_pulls(where, val_x, last, sums[1], val_attention, val_target)
    pull = jnp.concatenate([own_pull, send(own_pull, YHI)], axis=1)
    p_up, p_down = send(pull, UP), send(pull, DOWN)
    grads = value_grads(where, train_x, last, sums[0], attention, train_target, (own_pull,))
    grads = (grads, send(grads, CORE))

    def terms(zs, *waits):
        return skill_terms(where, train_x, other_x[zs], grads, zs, waits)

    pulls = {0: pull, 1: p_down, 7: p_up}
    sent, (up, down) = ring_step(1, terms((4,)), p_up, p_down)
    mine = terms((3, 5), sent)
    other_x[2, 6] = send(joined((picked,), (sent,))[0], CORE)
    columns = lax.all_to_all(copies(crossed, NX * NL, (sent,)), "tp", 0, 0)
    pulls[6], pulls[2] = up, down
    sent, (up, down) = ring_step(2, mine, up, down)
    mine = terms((2, 6), sent)
    pulls[5], pulls[3] = up, down
    sent, (up, down) = ring_step(3, mine, up, down)
    mine = terms((1, 7), sent)
    pulls[4] = up
    sent, (up, down) = ring_step(4, mine, up, down)
    near_pulls = stacked([pulls[dz] for dz in range(NZ)], (sent,))
    here = directions_of(where, val_skill, near_pulls, send(near_pulls, CORE), columns)
    there = send(here.astype(bf16), YHI)
    keep, give, local = local_transfer(terms((0,), sent, here), up, down, here, there)
    rows = lax.all_to_all(local, ("fsdp", "tp"), 0, 0)
    skill_grads = finish(keep, send(give, YHI))
    return (skill_grads, sum_rows(rows, (skill_grads,)))


def solution(mesh):
    placed = (
        P("fsdp", None),
        P("fsdp", "tp"),
        P("fsdp", "tp"),
        P("fsdp", "tp"),
        P(),
        P("fsdp", "tp"),
        P("fsdp", None),
        P("fsdp", "tp"),
        P("fsdp", "tp"),
        P("fsdp", "tp"),
        P(),
    )
    return jax.shard_map(
        on_device,
        mesh=mesh,
        in_specs=placed,
        out_specs=(P(None, "fsdp", "tp"), P()),
        check_vma=False,
    )
```
